32 devices in a mesh: prow: 8 (over z, x), pcol: 4 (over y, core).
Axes of the slice: x: 2, y: 2, z: 4, core: 2. Of those that a mesh axis runs over, the one named last changes fastest.
Arguments:
- b_panels: bfloat16 [3, 8, 4, 128, 512], P(None, 'prow', 'pcol'), may hold values from -6 to 6
- diag_inverse: bfloat16 [3, 8, 4, 128, 128], P(None, 'prow', 'pcol'), as said below
- l_blocks: bfloat16 [2, 8, 4, 4, 5, 128, 128], P(None, 'prow', 'pcol'), may hold values from -0.125 to 0.125
- block_cols: int32 [2, 8, 4, 4, 5], P(None, 'prow', 'pcol'), may hold values from 0 to 63, as said below
- live_counts: int32 [2, 8, 4, 4], P(None, 'prow', 'pcol'), may hold values from 0 to 5, as said below
Outputs:
- solution: bfloat16 [3, 8, 4, 128, 512], P(None, 'prow', 'pcol')
The draws below stay inside these ranges and needn't reach their ends.
Inputs may be any that keep to these rules, and one draw needn't show every extreme that they name: `block_cols`: for block row (l, r, q) and device column c, entries are l2 * 32 + p * 4 + c with l2 < l and 0 <= p < 8; the first live_counts[l - 1, r, c, q] slots are distinct. `live_counts`: at most min(5, l * 8) at level l; that bound is reached at every level. `diag_inverse`: lower triangular.
All inputs are finite; a program needn't handle non-finite values.
Results may differ from the reference program's by a relative error of at most 0.014.
Values may be sent and summed in bfloat16 or wider, within the bound.
No kernel may reach another device: no remote copies, remote signals or barrier semaphores. Data moves between devices by JAX's collectives and lax.ppermute only.
A program may use at most 128 MiB of HBM per device.

```python
import math
import jax
import jax.numpy as jnp
from jax import lax

B = 128
RHS = 512
LEVELS = 3
BLOCK_SLOT_COUNT = 5
NB_LEV = 32
N_PROW = 8
N_PCOL = 4


def draw_diag_inverse(key, part):
    first_key, secondary_key = jax.random.split(key)
    shape = (LEVELS, N_PROW, N_PCOL, B, B)
    lower_part = jax.random.normal(first_key, shape, jnp.float32) * (0.6 / math.sqrt(B))
    diagonal = jax.random.uniform(secondary_key, shape[:-1], jnp.float32, 0.7, 1.3)
    row_pos = jnp.arange(B)[:, None]
    col_pos = jnp.arange(B)[None, :]
    strict = jnp.where(row_pos > col_pos, lower_part, 0.0)
    return (strict + jnp.where(row_pos == col_pos, diagonal[..., :, None], 0.0)).astype(jnp.bfloat16)


def draw_block_cols(key, part):
    candidates = (LEVELS - 1) * N_PROW
    randomness_words = jax.random.randint(jax.random.fold_in(key, 11), (LEVELS - 1, N_PROW, N_PCOL, N_PCOL, candidates), 0, 1 << 20)
    candidate = jnp.arange(candidates).astype(jnp.int32)
    level_lookup = jnp.arange(1, LEVELS).astype(jnp.int32)[:, None, None, None, None]
    valid = candidate < level_lookup * N_PROW
    scores = jnp.where(valid, randomness_words * candidates + candidate, -1 - candidate)
    _, chosen = lax.top_k(scores, BLOCK_SLOT_COUNT)
    chosen = jnp.minimum(chosen.astype(jnp.int32), level_lookup * N_PROW - 1)
    prior_level = chosen // N_PROW
    prior_slot = chosen % N_PROW
    col_owner = jnp.arange(N_PCOL).astype(jnp.int32)[None, None, :, None, None]
    return (prior_level * NB_LEV + prior_slot * N_PCOL + col_owner).astype(jnp.int32)


def draw_live_counts(key, part):
    first_key, secondary_key = jax.random.split(jax.random.fold_in(key, 7))
    baseline_workload = jax.random.randint(first_key, (LEVELS - 1, N_PROW, N_PCOL, N_PCOL), 0, BLOCK_SLOT_COUNT + 1)
    column_extra_reward = jax.random.randint(secondary_key, (1, 1, N_PCOL, 1), 0, BLOCK_SLOT_COUNT)
    level_ceiling = jnp.minimum(BLOCK_SLOT_COUNT, jnp.arange(1, LEVELS).astype(jnp.int32) * N_PROW)[:, None, None, None]
    currently_active = jnp.minimum(jnp.minimum(baseline_workload + column_extra_reward, BLOCK_SLOT_COUNT), level_ceiling)
    currently_active = currently_active.at[:, 0, 0, 0].set(level_ceiling[:, 0, 0, 0])
    return currently_active.astype(jnp.int32)


def block_scale(key, extent, shards, least, largest):
    loudness, own = 1.0, jax.random.fold_in(key, 6)
    for axis_at, blocks in shards:
        draws = jnp.exp(jax.random.uniform(jax.random.fold_in(own, axis_at), (blocks,), jnp.float32, least / len(shards), largest / len(shards)))
        loudness = loudness * jnp.repeat(draws, extent[axis_at] // blocks).reshape([-1 if axis == axis_at else 1 for axis in range(len(extent))])
    return loudness


def centred(stream_key, shape, width, reach, cuts=(), held_as=jnp.bfloat16):
    result = jax.random.normal(stream_key, shape, jnp.float32) * width
    if len(cuts) > 0:
        result = block_scale(stream_key, shape, cuts, -0.22, 0.18) * result
    return jnp.clip(result, min=-reach, max=reach).astype(held_as)


def setup_inputs(seed: int = 0) -> dict:
    splits = jax.random.split(jax.random.key(seed), 6)
    b_panels = centred(splits[0], (LEVELS, N_PROW, N_PCOL, B, RHS), 1.0, 6.0, ((1, 8), (2, 4)))
    diag_inverse = draw_diag_inverse(jax.random.fold_in(splits[5], 71), 0)
    l_blocks = centred(splits[2], (LEVELS - 1, N_PROW, N_PCOL, N_PCOL, BLOCK_SLOT_COUNT, B, B), (B * N_PCOL * BLOCK_SLOT_COUNT) ** -0.5, 0.125, ((1, 8), (2, 4)))
    block_cols = draw_block_cols(jax.random.fold_in(splits[5], 71), 0)
    live_counts = draw_live_counts(jax.random.fold_in(splits[5], 71), 0)
    return dict(b_panels=b_panels, diag_inverse=diag_inverse, l_blocks=l_blocks, block_cols=block_cols, live_counts=live_counts)


def reference(b_panels, diag_inverse, l_blocks, block_cols, live_counts):
    proc_rows = N_PROW
    proc_cols = N_PCOL
    per_level = proc_rows * proc_cols
    solved = jnp.zeros((LEVELS * per_level, B, RHS), jnp.bfloat16)
    solutions = []
    for level_idx in range(LEVELS):
        right_part = b_panels[level_idx].astype(jnp.float32)
        if level_idx > 0:
            blocks = l_blocks[level_idx - 1]
            chosen = block_cols[level_idx - 1]
            currently_active = live_counts[level_idx - 1]

            def process_row(row_idx):
                def add_column(row_total, col_idx):
                    slot_mask = jnp.arange(BLOCK_SLOT_COUNT)[None, :] < currently_active[row_idx, col_idx][:, None]
                    masked = jnp.where(slot_mask[:, :, None, None], blocks[row_idx, col_idx], jnp.zeros((), jnp.bfloat16))
                    fetched = solved[chosen[row_idx, col_idx].astype(jnp.int32)].astype(jnp.float32)
                    partial_sum = jnp.einsum("jkab,jkbr->jar", masked.astype(jnp.float32), fetched,
                                             precision=lax.Precision.HIGHEST)
                    rounded = lax.optimization_barrier(partial_sum.astype(jnp.bfloat16))
                    return row_total + rounded.astype(jnp.float32), None

                start_total = jnp.zeros((proc_cols, B, RHS), jnp.float32)
                row_total, _ = lax.scan(add_column, start_total, jnp.arange(proc_cols).astype(jnp.int32))
                return row_total

            sums = lax.map(process_row, jnp.arange(proc_rows).astype(jnp.int32))
            right_part = right_part - sums
        resid = right_part.astype(jnp.bfloat16)
        solution = jnp.einsum("rcab,rcbs->rcas", diag_inverse[level_idx].astype(jnp.float32),
                              resid.astype(jnp.float32), precision=lax.Precision.HIGHEST).astype(jnp.bfloat16)
        solved = solved.at[level_idx * per_level:(level_idx + 1) * per_level].set(
            solution.reshape(per_level, B, RHS))
        solutions.append(solution)
    return jnp.stack(solutions)
```

```python
import functools

import jax
import jax.numpy as jnp
from jax import lax
from jax.experimental import pallas as pl
from jax.experimental.pallas import tpu as pltpu
from jax.sharding import PartitionSpec as P

LANES = 128
PAD_ROWS = 16
GATHER_BYTES = 16 * 2**20
VMEM_BYTES = 40 * 2**20


def vmem():
    return pl.BlockSpec(memory_space=pltpu.VMEM)


def smem():
    return pl.BlockSpec(memory_space=pltpu.SMEM)


def struct(shape, dtype=jnp.bfloat16):
    return jax.ShapeDtypeStruct(shape, dtype)


def params():
    return pltpu.CompilerParams(vmem_limit_bytes=VMEM_BYTES)


def solve_scattered(b_panels, diag_inverse, l_blocks, block_cols, live_counts):
    proc_rows = lax.axis_size("prow")
    proc_cols = lax.axis_size("pcol")
    per_level = proc_rows * proc_cols
    right_cols = b_panels[:, 0, 0]
    levels, block_size, front_width = right_cols.shape
    slot_count = l_blocks.shape[4]
    solved_cols = jnp.zeros((levels * proc_rows, block_size, front_width), jnp.bfloat16)
    solutions = []
    for level in range(levels):
        right_part = right_cols[level].astype(jnp.float32)
        if level > 0:
            chosen = block_cols[level - 1, 0, 0]
            active = live_counts[level - 1, 0, 0]
            local_index = chosen // per_level * proc_rows + chosen % per_level // proc_cols
            live = jnp.arange(slot_count)[None, :] < active[:, None]
            masked = jnp.where(live[:, :, None, None], l_blocks[level - 1, 0, 0], jnp.zeros((), jnp.bfloat16))
            partial = jnp.einsum(
                "jkab,jkbr->jar", masked, solved_cols[local_index], preferred_element_type=jnp.float32
            ).astype(jnp.bfloat16)
            row_total = lax.psum_scatter(partial, "pcol", scatter_dimension=0, tiled=True)
            right_part = right_part - row_total[0].astype(jnp.float32)
        resid = right_part.astype(jnp.bfloat16)
        solved = jnp.dot(diag_inverse[level, 0, 0], resid, preferred_element_type=jnp.float32).astype(jnp.bfloat16)
        solutions.append(solved)
        if level + 1 < levels:
            segment = lax.all_gather(solved[None], "prow", axis=0, tiled=True)
            solved_cols = lax.dynamic_update_slice_in_dim(solved_cols, segment, level * proc_rows, 0)
    return jnp.stack(solutions)[:, None, None]


def first_kernel(n, me_ref, b_ref, d_ref, full_ref, *piece_refs):
    me = me_ref[0]
    width = piece_refs[0].shape[1]
    full_ref[...] = jnp.dot(d_ref[...], b_ref[...], preferred_element_type=jnp.float32).astype(jnp.bfloat16)
    for j in range(n):
        start = pl.multiple_of((me ^ j) * width, LANES)
        piece_refs[j][...] = full_ref[:, pl.ds(start, width)]


def pack_kernel(n, me_ref, b_ref, d_ref, row_ref, *out_refs):
    me = me_ref[0]
    width = out_refs[0].shape[1]
    levels, size, _ = b_ref.shape
    for j in range(n):
        start = pl.multiple_of((me ^ j) * width, LANES)
        for level in range(1, levels):
            at = 2 * (level - 1) * size
            out_refs[j][at : at + size, :] = b_ref[level, :, pl.ds(start, width)]
            out_refs[j][at + size : at + 2 * size, :] = d_ref[level]
        out_refs[j][2 * (levels - 1) * size :, :] = row_ref[...]


def level_kernel(n, level, panels, me_ref, index_ref, *refs):
    x_refs = refs[:panels]
    l_refs = refs[panels : panels + n]
    p_refs = refs[panels + n : panels + 2 * n]
    out_ref = refs[panels + 2 * n]
    piece_refs = refs[panels + 2 * n + 1 : -1]
    known = refs[-1]
    me = me_ref[0]
    size, width = out_ref.shape[1:]
    slots = l_refs[0].shape[1]
    for s in range(panels):
        known[s] = x_refs[s][...]
    none = jnp.zeros((size, width), jnp.bfloat16)
    at = 2 * (level - 1) * size
    for jq in range(n):
        q = me ^ jq
        total = jnp.zeros((size, width), jnp.float32)
        for j in range(n):
            blocks, solved = [], []
            for k in range(slots):
                entry = index_ref[((level - 1) * n + j) * n * slots + q * slots + k]
                blocks.append(l_refs[j][q, k])
                solved.append(jnp.where(entry >= 0, known[jnp.maximum(entry, 0), j], none))
            total += jnp.dot(
                jnp.concatenate(blocks, axis=1), jnp.concatenate(solved, axis=0), preferred_element_type=jnp.float32
            )
        right = p_refs[jq][at : at + size, :].astype(jnp.float32)
        resid = (right - total).astype(jnp.bfloat16)
        inverse = p_refs[jq][at + size : at + 2 * size, :]
        value = jnp.dot(inverse, resid, preferred_element_type=jnp.float32).astype(jnp.bfloat16)
        out_ref[jq] = value
        piece_refs[jq][...] = value


def last_kernel(n, me_ref, full_ref, *refs):
    me = me_ref[0]
    out_ref = refs[-1]
    width = refs[0].shape[1]
    out_ref[0] = full_ref[...]
    for level in range(1, out_ref.shape[0]):
        for j in range(n):
            start = pl.multiple_of((me ^ j) * width, LANES)
            out_ref[level, :, pl.ds(start, width)] = refs[(level - 1) * n + j][...]


def swap(values, n):
    return [values[0]] + [lax.ppermute(values[j], "pcol", [(i, i ^ j) for i in range(n)]) for j in range(1, n)]


def ring_gather(value, cycle):
    m = len(cycle)
    to_next = [(cycle[i], cycle[(i + 1) % m]) for i in range(m)]
    to_last = [(b, a) for a, b in to_next]
    found = {0: value}
    behind = ahead = value
    for step in range(1, m // 2 + 1):
        behind = lax.ppermute(behind, "prow", to_next)
        found[m - step] = behind
        if step < m - step:
            ahead = lax.ppermute(ahead, "prow", to_last)
            found[step] = ahead
    return [found[d] for d in range(m)]


def solve_split(cycle, b_panels, diag_inverse, l_blocks, block_cols, live_counts):
    m = lax.axis_size("prow")
    n = lax.axis_size("pcol")
    levels, _, _, size, front = b_panels.shape
    slots = l_blocks.shape[4]
    width = front // n
    b = b_panels[:, 0, 0]
    inverse = diag_inverse[:, 0, 0]
    my_col = lax.axis_index("pcol")
    me = my_col.astype(jnp.int32)[None]

    full, *pieces = pl.pallas_call(
        functools.partial(first_kernel, n),
        out_shape=[struct((size, front))] + [struct((size, width))] * n,
        in_specs=[smem(), vmem(), vmem()],
        out_specs=[vmem()] * (n + 1),
        compiler_params=params(),
    )(me, b[0], inverse[0])
    solved = jnp.stack(swap(pieces, n))

    place = [cycle.index(p) for p in range(m)]
    chosen, counts = block_cols[:, 0, 0], live_counts[:, 0, 0]
    row_of = chosen % (m * n) // n
    place_of = sum(jnp.where(row_of == p, place[p], 0) for p in range(m))
    my_place = sum(jnp.where(lax.axis_index("prow") == p, place[p], 0) for p in range(m))
    entry = chosen // (m * n) * m + (place_of - my_place + m) % m
    live = jnp.arange(slots)[None, None, :] < counts[:, :, None]
    entry = jnp.where(live, entry, -1).reshape(-1).astype(jnp.bfloat16)
    row = jnp.zeros((PAD_ROWS * width,), jnp.bfloat16).at[: entry.size].set(entry).reshape(PAD_ROWS, width)

    packed = pl.pallas_call(
        functools.partial(pack_kernel, n),
        out_shape=[struct((2 * (levels - 1) * size + PAD_ROWS, width))] * n,
        in_specs=[smem(), vmem(), vmem(), vmem()],
        out_specs=[vmem()] * n,
        compiler_params=params(),
    )(me, b, inverse, row)
    packed = swap(packed, n)
    per_device = (levels - 1) * n * slots
    index = jnp.stack([p[-PAD_ROWS:].reshape(-1)[:per_device] for p in packed]).astype(jnp.int32)
    index = index.reshape(n, levels - 1, n * slots).transpose(1, 0, 2).reshape(-1)

    gathered = []
    for level in range(1, levels):
        held = [l_blocks[level - 1, 0, 0]]
        bit = n // 2
        while bit:
            swapped = [lax.ppermute(h, "pcol", [(i, i ^ bit) for i in range(n)]) for h in held]
            held = [v for pair in zip(held, swapped) for v in pair]
            bit //= 2
        gathered.append(held)

    panels, columns = [], []
    for level in range(1, levels):
        panels += ring_gather(solved, cycle)
        solved, *pieces = pl.pallas_call(
            functools.partial(level_kernel, n, level, len(panels)),
            out_shape=[struct((n, size, width))] + [struct((size, width))] * n,
            in_specs=[smem()] * 2 + [vmem()] * (len(panels) + 2 * n),
            out_specs=[vmem()] * (n + 1),
            scratch_shapes=[pltpu.VMEM((len(panels), n, size, width), jnp.bfloat16)],
            compiler_params=params(),
        )(me, index, *panels, *gathered[level - 1], *packed)
        columns += swap(pieces, n)

    out = pl.pallas_call(
        functools.partial(last_kernel, n),
        out_shape=struct((levels, size, front)),
        in_specs=[smem()] + [vmem()] * (1 + len(columns)),
        out_specs=vmem(),
        compiler_params=params(),
    )(me, full, *columns)
    return out[:, None, None]


def cycle_of(mesh):
    m = mesh.shape["prow"]
    names = list(mesh.axis_names)
    devices = mesh.devices.transpose([names.index("prow"), names.index("pcol")])[:, 0]
    spots = [tuple(getattr(d, "coords", None) or (i, 0, 0)) for i, d in enumerate(devices)]

    def near(a, b):
        return sum(abs(u - v) for u, v in zip(spots[a], spots[b])) == 1

    def extend(path):
        if len(path) == m:
            return path if near(path[-1], path[0]) else None
        for p in range(m):
            if p not in path and near(path[-1], p):
                found = extend(path + [p])
                if found:
                    return found
        return None

    return extend([0]) or list(range(m))


def solution(mesh):
    n = mesh.shape["pcol"]
    cycle = cycle_of(mesh)

    def shards(b_panels, diag_inverse, l_blocks, block_cols, live_counts):
        front = b_panels.shape[-1]
        splits = n & (n - 1) == 0 and front % (n * LANES) == 0
        if splits and n * l_blocks.size * l_blocks.dtype.itemsize <= GATHER_BYTES:
            return solve_split(cycle, b_panels, diag_inverse, l_blocks, block_cols, live_counts)
        return solve_scattered(b_panels, diag_inverse, l_blocks, block_cols, live_counts)

    return jax.shard_map(
        shards,
        mesh=mesh,
        in_specs=(
            P(None, "prow", "pcol", None, None),
            P(None, "prow", "pcol", None, None),
            P(None, "prow", "pcol", None, None, None, None),
            P(None, "prow", "pcol", None, None),
            P(None, "prow", "pcol", None),
        ),
        out_specs=P(None, "prow", "pcol", None, None),
        check_vma=False,
    )
```

```python
import functools

import jax
import jax.numpy as jnp
from jax import lax
from jax.experimental import pallas as pl
from jax.experimental.pallas import tpu as pltpu
from jax.sharding import PartitionSpec as P

LANES = 128
PAIR = 2
BLOCK_BYTES = 4 * 2**20
VMEM_BYTES = 16 * 2**20


def vmem():
    return pl.BlockSpec(memory_space=pltpu.VMEM)


def smem():
    return pl.BlockSpec(memory_space=pltpu.SMEM)


def anywhere():
    return pl.BlockSpec(memory_space=pl.ANY)


def in_hbm(value):
    return pltpu.with_memory_space_constraint(value, pltpu.HBM)


def struct(shape, dtype=jnp.bfloat16):
    return jax.ShapeDtypeStruct(shape, dtype)


def near(shape, dtype=jnp.bfloat16):
    return pltpu.VMEM(shape, dtype)


def params():
    return pltpu.CompilerParams(vmem_limit_bytes=VMEM_BYTES)


def solve_scattered(b_panels, diag_inverse, l_blocks, block_cols, live_counts):
    proc_rows = lax.axis_size("prow")
    proc_cols = lax.axis_size("pcol")
    per_level = proc_rows * proc_cols
    right_cols = b_panels[:, 0, 0]
    levels, block_size, front_width = right_cols.shape
    slot_count = l_blocks.shape[4]
    solved_cols = jnp.zeros((levels * proc_rows, block_size, front_width), jnp.bfloat16)
    solutions = []
    for level in range(levels):
        right_part = right_cols[level].astype(jnp.float32)
        if level > 0:
            chosen = block_cols[level - 1, 0, 0]
            active = live_counts[level - 1, 0, 0]
            local_index = chosen // per_level * proc_rows + chosen % per_level // proc_cols
            live = jnp.arange(slot_count)[None, :] < active[:, None]
            masked = jnp.where(live[:, :, None, None], l_blocks[level - 1, 0, 0], jnp.zeros((), jnp.bfloat16))
            partial = jnp.einsum(
                "jkab,jkbr->jar", masked, solved_cols[local_index], preferred_element_type=jnp.float32
            ).astype(jnp.bfloat16)
            row_total = lax.psum_scatter(partial, "pcol", scatter_dimension=0, tiled=True)
            right_part = right_part - row_total[0].astype(jnp.float32)
        resid = right_part.astype(jnp.bfloat16)
        solved = jnp.dot(diag_inverse[level, 0, 0], resid, preferred_element_type=jnp.float32).astype(jnp.bfloat16)
        solutions.append(solved)
        if level + 1 < levels:
            segment = lax.all_gather(solved[None], "prow", axis=0, tiled=True)
            solved_cols = lax.dynamic_update_slice_in_dim(solved_cols, segment, level * proc_rows, 0)
    return jnp.stack(solutions)[:, None, None]


def first_kernel(me_ref, b_ref, d_ref, full_ref, *refs):
    piece_refs, (b_buf, d_buf, sems) = refs[:PAIR], refs[PAIR:]
    copies = [
        pltpu.make_async_copy(b_ref.at[0, 0, 0], b_buf, sems.at[0]),
        pltpu.make_async_copy(d_ref.at[0, 0, 0], d_buf, sems.at[1]),
    ]
    for copy in copies:
        copy.start()
    for copy in copies:
        copy.wait()
    width = piece_refs[0].shape[1]
    full_ref[...] = jnp.dot(d_buf[...], b_buf[...], preferred_element_type=jnp.float32).astype(jnp.bfloat16)
    for j in range(PAIR):
        piece_refs[j][...] = full_ref[:, my_columns(me_ref[0] ^ j, width)]


def my_columns(me, width):
    return pl.ds(pl.multiple_of((me & 1) * width, LANES), width)


def gather_kernel(n, level, m, early, late, me_ref, index_ref, *refs):
    l_refs, refs = refs[:PAIR], refs[PAIR:]
    old_refs, refs = refs[: level - 1], refs[level - 1 :]
    x_refs, (total_ref, chosen_ref, known, buf, sems) = refs[:-5], refs[-5:]
    copies = [pltpu.make_async_copy(l_refs[j].at[level - 1, 0, 0], buf.at[j], sems.at[j]) for j in range(PAIR)]
    for copy in copies:
        copy.start()
    me = me_ref[0]
    size, width = total_ref.shape[1:]
    slots = buf.shape[2]
    base = (level - 1) * m
    for back in range(level - 1):
        known[back * m : (back + 1) * m] = old_refs[back][...]
    for d, x_ref in zip(early, x_refs):
        known[base + d] = x_ref[...]
    none = jnp.zeros((size, width), jnp.bfloat16)
    no_block = jnp.zeros((size, size), jnp.bfloat16)
    for j in range(PAIR):
        copies[j].wait()
        for jq in range(n):
            q = me ^ jq
            blocks, solved, chosen = [], [], [no_block] * len(late)
            for k in range(slots):
                entry = index_ref[((j * index_ref.shape[0] // (PAIR * n * slots) + level - 1) * n + q) * slots + k]
                use = entry >= 0
                block = buf[j, q, k]
                for i, d in enumerate(late):
                    is_late = entry == base + d
                    use = jnp.logical_and(use, entry != base + d)
                    chosen[i] = jnp.where(is_late, block, chosen[i])
                blocks.append(block)
                solved.append(jnp.where(use, known[jnp.maximum(entry, 0), j], none))
            product = jnp.dot(
                jnp.concatenate(blocks, axis=1), jnp.concatenate(solved, axis=0), preferred_element_type=jnp.float32
            )
            total_ref[jq] = product if j == 0 else total_ref[jq] + product
            for i in range(len(late)):
                at = (i * PAIR + j) * size
                chosen_ref[jq, :, at : at + size] = chosen[i]


def late_kernel(n, m, early, late, total_ref, chosen_ref, *refs):
    x_refs, refs = refs[: len(early)], refs[len(early) :]
    halves, refs = refs[:PAIR], refs[PAIR:]
    late_refs, refs = refs[: len(late) - 1], refs[len(late) - 1 :]
    panels_ref, keep_ref, send_refs = refs[0], refs[1], refs[2:]
    panels = []
    rest = iter(late_refs)
    for d in late:
        if d == m // 2:
            found = [halves[j][...] for j in range(PAIR)]
        else:
            ref = next(rest)
            found = [ref[j] for j in range(PAIR)]
        panels += found
        for j in range(PAIR):
            panels_ref[d, j] = found[j]
    panels = jnp.concatenate(panels, axis=0)
    for jq in reversed(range(n)):
        total = total_ref[jq] + jnp.dot(chosen_ref[jq], panels, preferred_element_type=jnp.float32)
        if jq < PAIR:
            keep_ref[jq] = total
        else:
            send_refs[jq // PAIR - 1][jq % PAIR] = total.astype(jnp.bfloat16)
    for d, x_ref in zip(early, x_refs):
        panels_ref[d] = x_ref[...]


def solve_kernel(level, me_ref, keep_ref, *refs):
    b_refs, d_refs, refs = refs[:PAIR], refs[PAIR : 2 * PAIR], refs[2 * PAIR :]
    other_refs, out_ref, piece_refs = refs[: -PAIR - 1], refs[-PAIR - 1], refs[-PAIR:]
    width = keep_ref.shape[2]
    columns = my_columns(me_ref[0], width)
    for j in range(PAIR):
        total = keep_ref[j]
        for other in other_refs:
            total += other[j].astype(jnp.float32)
        resid = (b_refs[j][level, 0, 0, :, columns].astype(jnp.float32) - total).astype(jnp.bfloat16)
        value = jnp.dot(d_refs[j][level, 0, 0], resid, preferred_element_type=jnp.float32).astype(jnp.bfloat16)
        out_ref[j] = value
        piece_refs[j][...] = value


def last_kernel(me_ref, full_ref, *refs):
    out_ref, sems = refs[-2:]
    width = refs[0].shape[1]
    copies = [pltpu.make_async_copy(full_ref, out_ref.at[0, 0, 0], sems.at[0])]
    for level in range(1, out_ref.shape[0]):
        for j in range(PAIR):
            at = (level - 1) * PAIR + j
            target = out_ref.at[level, 0, 0, :, my_columns(me_ref[0] ^ j, width)]
            copies.append(pltpu.make_async_copy(refs[at], target, sems.at[1 + at]))
    for copy in copies:
        copy.start()
    for copy in copies:
        copy.wait()


def after(value, *others):
    return lax.optimization_barrier((value, others))[0]


class Ring:
    def __init__(self, value, cycle):
        m = len(cycle)
        self.to_next = [(cycle[i], cycle[(i + 1) % m]) for i in range(m)]
        self.to_last = [(b, a) for a, b in self.to_next]
        self.size, self.step = m, 0
        self.found = {0: value}
        self.behind = self.ahead = value

    def advance(self):
        self.step += 1
        final = 2 * self.step == self.size
        if final:
            self.behind, self.ahead = self.behind[0], self.ahead[1]
        self.behind = lax.ppermute(self.behind, "prow", self.to_next)
        self.ahead = lax.ppermute(self.ahead, "prow", self.to_last)
        if not final:
            self.found[self.size - self.step] = self.behind
            self.found[self.step] = self.ahead


def solve_paired(cycle, b_panels, diag_inverse, l_blocks, block_cols, live_counts):
    m = lax.axis_size("prow")
    n = lax.axis_size("pcol")
    levels, _, _, size, front = b_panels.shape
    slots = l_blocks.shape[4]
    width = front // PAIR
    place = [cycle.index(p) for p in range(m)]
    my_place = sum(jnp.where(lax.axis_index("prow") == p, place[p], 0) for p in range(m))
    me = jnp.stack([lax.axis_index("pcol"), my_place]).astype(jnp.int32)

    def send(value, bits):
        return lax.ppermute(value, "pcol", [(i, i ^ bits) for i in range(n)])

    full, *pieces = pl.pallas_call(
        first_kernel,
        out_shape=[near((size, front))] + [near((size, width))] * PAIR,
        in_specs=[smem()] + [anywhere()] * 2,
        out_specs=[vmem()] * (1 + PAIR),
        scratch_shapes=[
            pltpu.VMEM((size, front), jnp.bfloat16),
            pltpu.VMEM((size, size), jnp.bfloat16),
            pltpu.SemaphoreType.DMA((2,)),
        ],
        compiler_params=params(),
    )(me, in_hbm(b_panels), in_hbm(diag_inverse))
    solved = jnp.stack([pieces[0], send(pieces[1], 1)])

    chosen, counts = block_cols[:, 0, 0], live_counts[:, 0, 0]
    row_of = chosen % (m * n) // n
    place_of = sum(jnp.where(row_of == p, place[p], 0) for p in range(m))
    entry = chosen // (m * n) * m + (place_of - my_place + m) % m
    entry = jnp.where(jnp.arange(slots)[None, None, :] < counts[:, :, None], entry, -1).reshape(-1)
    index = jnp.concatenate([entry, send(after(entry, solved), 1)])

    b, inverse, blocks = [[v, send(after(v, solved), 1)] for v in (b_panels, diag_inverse, l_blocks)]
    late = [d for d in range(1, m) if min(d, m - d) >= m // 2 - 1]
    early = [d for d in range(m) if d not in late]
    columns, kept = [], []
    for level in range(1, levels):
        ring = Ring(solved, cycle)
        for step in range(m // 2):
            ring.advance()
        total, chosen = pl.pallas_call(
            functools.partial(gather_kernel, n, level, m, early, late),
            out_shape=[near((n, size, width), jnp.float32), near((n, size, len(late) * PAIR * size))],
            in_specs=[smem()] * 2 + [anywhere()] * PAIR + [vmem()] * (len(kept) + len(early)),
            out_specs=[vmem()] * 2,
            scratch_shapes=[
                pltpu.VMEM((level * m, PAIR, size, width), jnp.bfloat16),
                pltpu.VMEM((PAIR, n, slots, size, size), jnp.bfloat16),
                pltpu.SemaphoreType.DMA((PAIR,)),
            ],
            compiler_params=params(),
        )(me, index, *[in_hbm(v) for v in blocks], *kept, *[ring.found[d] for d in early])
        panels, keep, *away = pl.pallas_call(
            functools.partial(late_kernel, n, m, early, late),
            out_shape=[near((m, PAIR, size, width)), near((PAIR, size, width), jnp.float32)]
            + [near((PAIR, size, width))] * (n // PAIR - 1),
            in_specs=[vmem()] * (2 + len(early) + PAIR + len(late) - 1),
            out_specs=[vmem()] * (1 + n // PAIR),
            compiler_params=params(),
        )(
            total,
            chosen,
            *[ring.found[d] for d in early],
            ring.behind,
            ring.ahead,
            *[ring.found[d] for d in late if d != m // 2],
        )
        kept.append(panels)
        others = [send(v, PAIR * (h + 1)) for h, v in enumerate(away)]
        solved, *pieces = pl.pallas_call(
            functools.partial(solve_kernel, level),
            out_shape=[near((PAIR, size, width))] + [near((size, width))] * PAIR,
            in_specs=[smem()] + [vmem()] * (1 + 2 * PAIR + len(others)),
            out_specs=[vmem()] * (1 + PAIR),
            compiler_params=params(),
        )(me, keep, *b, *inverse, *others)
        columns += [pieces[0], send(pieces[1], 1)]

    return pl.pallas_call(
        last_kernel,
        out_shape=struct(b_panels.shape),
        in_specs=[smem()] + [vmem()] * (1 + len(columns)),
        out_specs=anywhere(),
        scratch_shapes=[pltpu.SemaphoreType.DMA((1 + len(columns),))],
        compiler_params=params(),
    )(me, full, *columns)


def cycle_of(mesh):
    m = mesh.shape["prow"]
    names = list(mesh.axis_names)
    devices = mesh.devices.transpose([names.index("prow"), names.index("pcol")])[:, 0]
    spots = [tuple(getattr(d, "coords", None) or (i, 0, 0)) for i, d in enumerate(devices)]

    def near(a, b):
        return sum(abs(u - v) for u, v in zip(spots[a], spots[b])) == 1

    def extend(path):
        if len(path) == m:
            return path if near(path[-1], path[0]) else None
        for p in range(m):
            if p not in path and near(path[-1], p):
                found = extend(path + [p])
                if found:
                    return found
        return None

    return extend([0]) or list(range(m))


def solution(mesh):
    n = mesh.shape["pcol"]
    cycle = cycle_of(mesh)

    def shards(b_panels, diag_inverse, l_blocks, block_cols, live_counts):
        front = b_panels.shape[-1]
        rows = mesh.shape["prow"]
        paired = n & (n - 1) == 0 and n >= PAIR and rows % 2 == 0 and front % (PAIR * LANES) == 0
        if paired and l_blocks.size * l_blocks.dtype.itemsize <= BLOCK_BYTES:
            return solve_paired(cycle, b_panels, diag_inverse, l_blocks, block_cols, live_counts)
        return solve_scattered(b_panels, diag_inverse, l_blocks, block_cols, live_counts)

    return jax.shard_map(
        shards,
        mesh=mesh,
        in_specs=(
            P(None, "prow", "pcol", None, None),
            P(None, "prow", "pcol", None, None),
            P(None, "prow", "pcol", None, None, None, None),
            P(None, "prow", "pcol", None, None),
            P(None, "prow", "pcol", None),
        ),
        out_specs=P(None, "prow", "pcol", None, None),
        check_vma=False,
    )
```

```python
import functools

import jax
import jax.numpy as jnp
from jax import lax
from jax.experimental import pallas as pl
from jax.experimental.pallas import tpu as pltpu
from jax.sharding import PartitionSpec as P

LANES = 128
PAIR = 2
BLOCK_BYTES = 4 * 2**20
VMEM_BYTES = 16 * 2**20


def vmem():
    return pl.BlockSpec(memory_space=pltpu.VMEM)


def smem():
    return pl.BlockSpec(memory_space=pltpu.SMEM)


def anywhere():
    return pl.BlockSpec(memory_space=pl.ANY)


def in_hbm(value):
    return pltpu.with_memory_space_constraint(value, pltpu.HBM)


def struct(shape, dtype=jnp.bfloat16):
    return jax.ShapeDtypeStruct(shape, dtype)


def near(shape, dtype=jnp.bfloat16):
    return pltpu.VMEM(shape, dtype)


def params():
    return pltpu.CompilerParams(vmem_limit_bytes=VMEM_BYTES)


def solve_scattered(b_panels, diag_inverse, l_blocks, block_cols, live_counts):
    proc_rows = lax.axis_size("prow")
    proc_cols = lax.axis_size("pcol")
    per_level = proc_rows * proc_cols
    right_cols = b_panels[:, 0, 0]
    levels, block_size, front_width = right_cols.shape
    slot_count = l_blocks.shape[4]
    solved_cols = jnp.zeros((levels * proc_rows, block_size, front_width), jnp.bfloat16)
    solutions = []
    for level in range(levels):
        right_part = right_cols[level].astype(jnp.float32)
        if level > 0:
            chosen = block_cols[level - 1, 0, 0]
            active = live_counts[level - 1, 0, 0]
            local_index = chosen // per_level * proc_rows + chosen % per_level // proc_cols
            live = jnp.arange(slot_count)[None, :] < active[:, None]
            masked = jnp.where(live[:, :, None, None], l_blocks[level - 1, 0, 0], jnp.zeros((), jnp.bfloat16))
            partial = jnp.einsum(
                "jkab,jkbr->jar", masked, solved_cols[local_index], preferred_element_type=jnp.float32
            ).astype(jnp.bfloat16)
            row_total = lax.psum_scatter(partial, "pcol", scatter_dimension=0, tiled=True)
            right_part = right_part - row_total[0].astype(jnp.float32)
        resid = right_part.astype(jnp.bfloat16)
        solved = jnp.dot(diag_inverse[level, 0, 0], resid, preferred_element_type=jnp.float32).astype(jnp.bfloat16)
        solutions.append(solved)
        if level + 1 < levels:
            segment = lax.all_gather(solved[None], "prow", axis=0, tiled=True)
            solved_cols = lax.dynamic_update_slice_in_dim(solved_cols, segment, level * proc_rows, 0)
    return jnp.stack(solutions)[:, None, None]


def first_kernel(n, m, place, me_ref, counts_ref, cols_ref, b_ref, d_ref, full_ref, index_ref, *refs):
    piece_refs, (b_buf, d_buf, count_ref, col_ref, sems) = refs[:PAIR], refs[PAIR:]
    copies = [
        pltpu.make_async_copy(counts_ref, count_ref, sems.at[0]),
        pltpu.make_async_copy(cols_ref, col_ref, sems.at[1]),
        pltpu.make_async_copy(b_ref.at[0, 0, 0], b_buf, sems.at[2]),
        pltpu.make_async_copy(d_ref.at[0, 0, 0], d_buf, sems.at[3]),
    ]
    for copy in copies:
        copy.start()
    for copy in copies[2:]:
        copy.wait()
    me, my_place = me_ref[0], me_ref[1]
    width = piece_refs[0].shape[1]
    full_ref[...] = jnp.dot(d_buf[...], b_buf[...], preferred_element_type=jnp.float32).astype(jnp.bfloat16)
    for j in range(PAIR):
        piece_refs[j][...] = full_ref[:, my_columns(me ^ j, width)]
    for copy in copies[:2]:
        copy.wait()
    levels, slots = col_ref.shape[0] + 1, col_ref.shape[-1]
    row_at = lax.broadcasted_iota(jnp.int32, (n, slots), 0)
    slot_at = lax.broadcasted_iota(jnp.int32, (n, slots), 1)
    index_ref[...] = jnp.zeros_like(index_ref)
    for level in range(1, levels):
        rest = col_ref[level - 1, 0, 0]
        first = jnp.zeros_like(rest)
        for _ in range(1, level):
            past = rest >= m * n
            first += jnp.where(past, m, 0)
            rest -= jnp.where(past, m * n, 0)
        ahead = place[0] - my_place + jnp.zeros_like(rest)
        for p in range(1, m):
            ahead += jnp.where(rest >= p * n, place[p] - place[p - 1], 0)
        entry = first + jnp.where(ahead < 0, ahead + m, ahead)
        count = jnp.zeros_like(rest)
        for q in range(n):
            count = jnp.where(row_at == q, count_ref[level - 1, 0, 0, q], count)
        index_ref[(level - 1) * n : level * n, :slots] = jnp.where(slot_at < count, entry, -1)


def my_columns(me, width):
    return pl.ds(pl.multiple_of((me & 1) * width, LANES), width)


def gather_kernel(n, level, m, early, late, me_ref, *refs):
    index_refs, l_refs, refs = refs[:PAIR], refs[PAIR : 2 * PAIR], refs[2 * PAIR :]
    old_refs, refs = refs[: level - 1], refs[level - 1 :]
    x_refs, (total_ref, chosen_ref, known, own, sem) = refs[:-5], refs[-5:]
    copy = pltpu.make_async_copy(l_refs[0].at[level - 1, 0, 0], own, sem)
    copy.start()
    me = me_ref[0]
    size, width = total_ref.shape[1:]
    slots = l_refs[0].shape[4]
    base = (level - 1) * m
    for back in range(level - 1):
        known[back * m : (back + 1) * m] = old_refs[back][...]
    for d, x_ref in zip(early, x_refs):
        known[base + d] = x_ref[...]
    none = jnp.zeros((size, width), jnp.bfloat16)
    no_block = jnp.zeros((size, size), jnp.bfloat16)
    for j in reversed(range(PAIR)):
        if j == 0:
            copy.wait()
        for jq in range(n):
            q = me ^ jq
            blocks, solved, chosen = [], [], [no_block] * len(late)
            for k in range(slots):
                entry = index_refs[j][(level - 1) * n + q, k]
                use = entry >= 0
                block = l_refs[j][level - 1, 0, 0, q, k] if j else own[q, k]
                for i, d in enumerate(late):
                    is_late = entry == base + d
                    use = jnp.logical_and(use, entry != base + d)
                    chosen[i] = jnp.where(is_late, block, chosen[i])
                blocks.append(block)
                solved.append(jnp.where(use, known[jnp.maximum(entry, 0), j], none))
            product = jnp.dot(
                jnp.concatenate(blocks, axis=1), jnp.concatenate(solved, axis=0), preferred_element_type=jnp.float32
            )
            total_ref[jq] = product if j == PAIR - 1 else total_ref[jq] + product
            for i in range(len(late)):
                at = (i * PAIR + j) * size
                chosen_ref[jq, :, at : at + size] = chosen[i]


def late_kernel(n, early, late, final, total_ref, chosen_ref, *refs):
    x_refs, refs = refs[: len(early)], refs[len(early) :]
    late_refs, refs = refs[: len(late)], refs[len(late) :]
    if not final:
        panels_ref, refs = refs[0], refs[1:]
    keep_ref, send_refs = refs[0], refs[1:]
    for d, x_ref in zip(late if not final else (), late_refs):
        panels_ref[d] = x_ref[...]
    panels = jnp.concatenate([x_ref[j] for x_ref in late_refs for j in range(PAIR)], axis=0)
    rows = 1 if final else PAIR
    for jq in reversed(range(n)):
        total = total_ref[jq] + jnp.dot(chosen_ref[jq], panels, preferred_element_type=jnp.float32)
        if jq < rows:
            keep_ref[jq] = total
        else:
            send_refs[jq // rows - 1][jq % rows] = total.astype(jnp.bfloat16)
    if not final:
        for d, x_ref in zip(early, x_refs):
            panels_ref[d] = x_ref[...]


def solve_kernel(level, me_ref, keep_ref, *refs):
    b_refs, d_refs, refs = refs[:PAIR], refs[PAIR : 2 * PAIR], refs[2 * PAIR :]
    other_refs, out_ref, piece_refs = refs[: -PAIR - 1], refs[-PAIR - 1], refs[-PAIR:]
    width = keep_ref.shape[2]
    columns = my_columns(me_ref[0], width)
    for j in range(PAIR):
        total = keep_ref[j]
        for other in other_refs:
            total += other[j].astype(jnp.float32)
        resid = (b_refs[j][level, 0, 0, :, columns].astype(jnp.float32) - total).astype(jnp.bfloat16)
        value = jnp.dot(d_refs[j][level, 0, 0], resid, preferred_element_type=jnp.float32).astype(jnp.bfloat16)
        out_ref[j] = value
        piece_refs[j][...] = value


def last_kernel(n, me_ref, b_ref, d_ref, keep_ref, *refs):
    other_refs, refs = refs[: n - 1], refs[n - 1 :]
    full_ref, refs = refs[0], refs[1:]
    piece_refs, (out_ref, buf, sems) = refs[:-3], refs[-3:]
    me = me_ref[0]
    width = keep_ref.shape[2]
    levels = out_ref.shape[0]
    copies = [pltpu.make_async_copy(full_ref, out_ref.at[0, 0, 0], sems.at[0])]
    for i, ref in enumerate(piece_refs):
        target = out_ref.at[1 + i // PAIR, 0, 0, :, my_columns(me ^ (i % PAIR), width)]
        copies.append(pltpu.make_async_copy(ref, target, sems.at[1 + i]))
    for copy in copies:
        copy.start()
    for j in range(PAIR):
        total = keep_ref[0] if j == 0 else jnp.zeros_like(keep_ref[0])
        for jq in range(1, n):
            if jq % PAIR == j:
                total += other_refs[jq - 1][0].astype(jnp.float32)
        columns = my_columns(me ^ j, width)
        resid = (b_ref[levels - 1, 0, 0, :, columns].astype(jnp.float32) - total).astype(jnp.bfloat16)
        value = jnp.dot(d_ref[levels - 1, 0, 0], resid, preferred_element_type=jnp.float32)
        buf[:, columns] = value.astype(jnp.bfloat16)
        target = out_ref.at[levels - 1, 0, 0, :, columns]
        copies.append(pltpu.make_async_copy(buf.at[:, columns], target, sems.at[1 + len(piece_refs) + j]))
        copies[-1].start()
    for copy in copies:
        copy.wait()


def after(value, *others):
    return lax.optimization_barrier((value, others))[0]


class Ring:
    def __init__(self, value, cycle):
        m = len(cycle)
        self.to_next = [(cycle[i], cycle[(i + 1) % m]) for i in range(m)]
        self.to_last = [(b, a) for a, b in self.to_next]
        self.size, self.step = m, 0
        self.found = {0: value}
        self.behind = self.ahead = value

    def advance(self):
        self.step += 1
        self.behind = lax.ppermute(self.behind, "prow", self.to_next)
        self.found[self.size - self.step] = self.behind
        if self.step < self.size - self.step:
            self.ahead = lax.ppermute(self.ahead, "prow", self.to_last)
            self.found[self.step] = self.ahead


def solve_paired(cycle, b_panels, diag_inverse, l_blocks, block_cols, live_counts):
    m = lax.axis_size("prow")
    n = lax.axis_size("pcol")
    levels, _, _, size, front = b_panels.shape
    slots = l_blocks.shape[4]
    width = front // PAIR
    place = [cycle.index(p) for p in range(m)]
    my_place = sum(jnp.where(lax.axis_index("prow") == p, place[p], 0) for p in range(m))
    me = jnp.stack([lax.axis_index("pcol"), my_place]).astype(jnp.int32)

    def send(value, bits):
        return lax.ppermute(value, "pcol", [(i, i ^ bits) for i in range(n)])

    index_shape = (-(-(levels - 1) * n // 8) * 8, LANES)

    full, index, *pieces = pl.pallas_call(
        functools.partial(first_kernel, n, m, place),
        out_shape=[near((size, front)), near(index_shape, jnp.int32)] + [near((size, width))] * PAIR,
        in_specs=[smem()] + [anywhere()] * 4,
        out_specs=[vmem()] * (2 + PAIR),
        scratch_shapes=[
            pltpu.VMEM((size, front), jnp.bfloat16),
            pltpu.VMEM((size, size), jnp.bfloat16),
            pltpu.SMEM(live_counts.shape, jnp.int32),
            pltpu.VMEM(block_cols.shape, jnp.int32),
            pltpu.SemaphoreType.DMA((4,)),
        ],
        compiler_params=params(),
    )(me, *[in_hbm(v) for v in (live_counts, block_cols, b_panels, diag_inverse)])
    index = [index, send(index, 1)]
    solved = after(jnp.stack([pieces[0], send(pieces[1], 1)]), index[1])
    b, inverse, blocks = [[v, send(after(v, solved), 1)] for v in (b_panels, diag_inverse, l_blocks)]
    blocks[0] = in_hbm(l_blocks)

    late = [d for d in range(1, m) if min(d, m - d) >= m // 2 - 1]
    early = [d for d in range(m) if d not in late]
    columns, kept = [], []
    for level in range(1, levels):
        final = level == levels - 1
        ring = Ring(solved, cycle)
        for _ in range(m // 2):
            ring.advance()
        total, chosen = pl.pallas_call(
            functools.partial(gather_kernel, n, level, m, early, late),
            out_shape=[near((n, size, width), jnp.float32), near((n, size, len(late) * PAIR * size))],
            in_specs=[smem()] * (1 + PAIR) + [anywhere()] + [vmem()] * (PAIR - 1 + len(kept) + len(early)),
            out_specs=[vmem()] * 2,
            scratch_shapes=[
                pltpu.VMEM((level * m, PAIR, size, width), jnp.bfloat16),
                pltpu.VMEM(l_blocks.shape[3:], jnp.bfloat16),
                pltpu.SemaphoreType.DMA,
            ],
            compiler_params=params(),
        )(me, *index, *blocks, *kept, *[ring.found[d] for d in early])
        rows = 1 if final else PAIR
        out_shape = [near((rows, size, width), jnp.float32)] + [near((rows, size, width))] * (n // rows - 1)
        if not final:
            out_shape = [near((m, PAIR, size, width))] + out_shape
        found = pl.pallas_call(
            functools.partial(late_kernel, n, early, late, final),
            out_shape=out_shape,
            in_specs=[vmem()] * (2 + m),
            out_specs=[vmem()] * len(out_shape),
            compiler_params=params(),
        )(
            total,
            chosen,
            *[ring.found[d] for d in early + late],
        )
        if not final:
            panels, *found = found
            kept.append(panels)
        keep, *away = found
        others = [send(v, rows * (h + 1)) for h, v in enumerate(away)]
        if final:
            columns = [send(after(v, keep), 1) if i % PAIR else v for i, v in enumerate(columns)]
            break
        solved, *pieces = pl.pallas_call(
            functools.partial(solve_kernel, level),
            out_shape=[near((PAIR, size, width))] + [near((size, width))] * PAIR,
            in_specs=[smem()] + [vmem()] * (1 + 2 * PAIR + len(others)),
            out_specs=[vmem()] * (1 + PAIR),
            compiler_params=params(),
        )(me, keep, *b, *inverse, *others)
        columns += pieces

    return pl.pallas_call(
        functools.partial(last_kernel, n),
        out_shape=struct(b_panels.shape),
        in_specs=[smem()] + [vmem()] * (4 + len(others) + len(columns)),
        out_specs=anywhere(),
        scratch_shapes=[
            pltpu.VMEM((size, front), jnp.bfloat16),
            pltpu.SemaphoreType.DMA((1 + PAIR + len(columns),)),
        ],
        compiler_params=params(),
    )(me, b_panels, diag_inverse, keep, *others, full, *columns)


def cycle_of(mesh):
    m = mesh.shape["prow"]
    names = list(mesh.axis_names)
    devices = mesh.devices.transpose([names.index("prow"), names.index("pcol")])[:, 0]
    spots = [tuple(getattr(d, "coords", None) or (i, 0, 0)) for i, d in enumerate(devices)]

    def near(a, b):
        return sum(abs(u - v) for u, v in zip(spots[a], spots[b])) == 1

    def extend(path):
        if len(path) == m:
            return path if near(path[-1], path[0]) else None
        for p in range(m):
            if p not in path and near(path[-1], p):
                found = extend(path + [p])
                if found:
                    return found
        return None

    return extend([0]) or list(range(m))


def solution(mesh):
    n = mesh.shape["pcol"]
    cycle = cycle_of(mesh)

    def shards(b_panels, diag_inverse, l_blocks, block_cols, live_counts):
        front = b_panels.shape[-1]
        rows = mesh.shape["prow"]
        paired = n & (n - 1) == 0 and n >= PAIR and rows % 2 == 0 and rows > 2 and front % (PAIR * LANES) == 0
        paired = paired and b_panels.shape[0] > 1
        if paired and l_blocks.size * l_blocks.dtype.itemsize <= BLOCK_BYTES:
            return solve_paired(cycle, b_panels, diag_inverse, l_blocks, block_cols, live_counts)
        return solve_scattered(b_panels, diag_inverse, l_blocks, block_cols, live_counts)

    return jax.shard_map(
        shards,
        mesh=mesh,
        in_specs=(
            P(None, "prow", "pcol", None, None),
            P(None, "prow", "pcol", None, None),
            P(None, "prow", "pcol", None, None, None, None),
            P(None, "prow", "pcol", None, None),
            P(None, "prow", "pcol", None),
        ),
        out_specs=P(None, "prow", "pcol", None, None),
        check_vma=False,
    )
```

```python
import functools

import jax
import jax.numpy as jnp
from jax import lax
from jax.experimental import pallas as pl
from jax.experimental.pallas import tpu as pltpu
from jax.sharding import PartitionSpec as P

LANES = 128
PAIR = 2
BLOCK_BYTES = 4 * 2**20
VMEM_BYTES = 16 * 2**20


def vmem():
    return pl.BlockSpec(memory_space=pltpu.VMEM)


def smem():
    return pl.BlockSpec(memory_space=pltpu.SMEM)


def anywhere():
    return pl.BlockSpec(memory_space=pl.ANY)


def in_hbm(value):
    return pltpu.with_memory_space_constraint(value, pltpu.HBM)


def struct(shape, dtype=jnp.bfloat16):
    return jax.ShapeDtypeStruct(shape, dtype)


def near(shape, dtype=jnp.bfloat16):
    return pltpu.VMEM(shape, dtype)


def params():
    return pltpu.CompilerParams(vmem_limit_bytes=VMEM_BYTES)


def solve_scattered(b_panels, diag_inverse, l_blocks, block_cols, live_counts):
    proc_rows = lax.axis_size("prow")
    proc_cols = lax.axis_size("pcol")
    per_level = proc_rows * proc_cols
    right_cols = b_panels[:, 0, 0]
    levels, block_size, front_width = right_cols.shape
    slot_count = l_blocks.shape[4]
    solved_cols = jnp.zeros((levels * proc_rows, block_size, front_width), jnp.bfloat16)
    solutions = []
    for level in range(levels):
        right_part = right_cols[level].astype(jnp.float32)
        if level > 0:
            chosen = block_cols[level - 1, 0, 0]
            active = live_counts[level - 1, 0, 0]
            local_index = chosen // per_level * proc_rows + chosen % per_level // proc_cols
            live = jnp.arange(slot_count)[None, :] < active[:, None]
            masked = jnp.where(live[:, :, None, None], l_blocks[level - 1, 0, 0], jnp.zeros((), jnp.bfloat16))
            partial = jnp.einsum(
                "jkab,jkbr->jar", masked, solved_cols[local_index], preferred_element_type=jnp.float32
            ).astype(jnp.bfloat16)
            row_total = lax.psum_scatter(partial, "pcol", scatter_dimension=0, tiled=True)
            right_part = right_part - row_total[0].astype(jnp.float32)
        resid = right_part.astype(jnp.bfloat16)
        solved = jnp.dot(diag_inverse[level, 0, 0], resid, preferred_element_type=jnp.float32).astype(jnp.bfloat16)
        solutions.append(solved)
        if level + 1 < levels:
            segment = lax.all_gather(solved[None], "prow", axis=0, tiled=True)
            solved_cols = lax.dynamic_update_slice_in_dim(solved_cols, segment, level * proc_rows, 0)
    return jnp.stack(solutions)[:, None, None]


def first_kernel(n, m, place, me_ref, counts_ref, cols_ref, b_ref, d_ref, full_ref, index_ref, own_ref, away_ref, *refs):
    b_buf, d_buf, count_ref, col_ref, sems = refs
    middle = b_buf.shape[0]
    copies = [
        pltpu.make_async_copy(counts_ref, count_ref, sems.at[0]),
        pltpu.make_async_copy(cols_ref, col_ref, sems.at[1]),
        pltpu.make_async_copy(d_ref.at[pl.ds(0, middle), 0, 0], d_buf, sems.at[2]),
        pltpu.make_async_copy(b_ref.at[pl.ds(0, middle), 0, 0], b_buf, sems.at[3]),
    ]
    for copy in copies:
        copy.start()
    me, my_place = me_ref[0], me_ref[1]
    size, width = own_ref.shape
    for copy in copies[2:]:
        copy.wait()
    full_ref[...] = jnp.dot(d_buf[0], b_buf[0], preferred_element_type=jnp.float32).astype(jnp.bfloat16)
    own_ref[...] = full_ref[:, my_columns(me, width)]
    away_ref[:size, :] = full_ref[:, my_columns(me ^ 1, width)]
    for level in range(1, middle):
        at = (2 * level - 1) * size
        away_ref[at : at + size, :] = b_buf[level, :, my_columns(me ^ 1, width)]
        away_ref[at + size : at + 2 * size, :size] = d_buf[level]
        away_ref[at + size : at + 2 * size, size:] = jnp.zeros((size, width - size), jnp.bfloat16)
    for copy in copies[:2]:
        copy.wait()
    levels, slots = col_ref.shape[0] + 1, col_ref.shape[-1]
    row_at = lax.broadcasted_iota(jnp.int32, (n, slots), 0)
    slot_at = lax.broadcasted_iota(jnp.int32, (n, slots), 1)
    index_ref[...] = jnp.zeros_like(index_ref)
    for level in range(1, levels):
        rest = col_ref[level - 1, 0, 0]
        first = jnp.zeros_like(rest)
        for _ in range(1, level):
            past = rest >= m * n
            first += jnp.where(past, m, 0)
            rest -= jnp.where(past, m * n, 0)
        ahead = place[0] - my_place + jnp.zeros_like(rest)
        for p in range(1, m):
            ahead += jnp.where(rest >= p * n, place[p] - place[p - 1], 0)
        entry = first + jnp.where(ahead < 0, ahead + m, ahead)
        count = jnp.zeros_like(rest)
        for q in range(n):
            count = jnp.where(row_at == q, count_ref[level - 1, 0, 0, q], count)
        index_ref[(level - 1) * n : level * n, :slots] = jnp.where(slot_at < count, entry, -1)


def my_columns(me, width):
    return pl.ds(pl.multiple_of((me & 1) * width, LANES), width)


def gather_kernel(n, level, m, early, late, me_ref, *refs):
    index_refs, l_refs, refs = refs[:PAIR], refs[PAIR : 2 * PAIR], refs[2 * PAIR :]
    old_refs, refs = refs[: level - 1], refs[level - 1 :]
    x_refs, (total_ref, chosen_ref, known, own, sem) = refs[:-5], refs[-5:]
    copy = pltpu.make_async_copy(l_refs[0].at[level - 1, 0, 0], own, sem)
    copy.start()
    me = me_ref[0]
    size, width = total_ref.shape[1:]
    slots = l_refs[0].shape[4]
    base = (level - 1) * m
    for back in range(level - 1):
        known[back * m : (back + 1) * m] = old_refs[back][...]
    for d, x_ref in zip(early, x_refs):
        known[base + d] = x_ref[...]
    none = jnp.zeros((size, width), jnp.bfloat16)
    no_block = jnp.zeros((size, size), jnp.bfloat16)
    for j in reversed(range(PAIR)):
        if j == 0:
            copy.wait()
        for jq in range(n):
            q = me ^ jq
            blocks, solved, chosen = [], [], [no_block] * len(late)
            for k in range(slots):
                entry = index_refs[j][(level - 1) * n + q, k]
                use = entry >= 0
                block = l_refs[j][level - 1, 0, 0, q, k] if j else own[q, k]
                for i, d in enumerate(late):
                    is_late = entry == base + d
                    use = jnp.logical_and(use, entry != base + d)
                    chosen[i] = jnp.where(is_late, block, chosen[i])
                blocks.append(block)
                solved.append(jnp.where(use, known[jnp.maximum(entry, 0), j], none))
            product = jnp.dot(
                jnp.concatenate(blocks, axis=1), jnp.concatenate(solved, axis=0), preferred_element_type=jnp.float32
            )
            total_ref[jq] = product if j == PAIR - 1 else total_ref[jq] + product
            for i in range(len(late)):
                at = (i * PAIR + j) * size
                chosen_ref[jq, :, at : at + size] = chosen[i]


def late_kernel(n, early, late, final, total_ref, chosen_ref, *refs):
    x_refs, refs = refs[: len(early)], refs[len(early) :]
    late_refs, refs = refs[: len(late)], refs[len(late) :]
    if not final:
        panels_ref, refs = refs[0], refs[1:]
    keep_ref, send_refs = refs[0], refs[1:]
    for d, x_ref in zip(late if not final else (), late_refs):
        panels_ref[d] = x_ref[...]
    panels = jnp.concatenate([x_ref[j] for x_ref in late_refs for j in range(PAIR)], axis=0)
    rows = 1 if final else PAIR
    for jq in reversed(range(n)):
        total = total_ref[jq] + jnp.dot(chosen_ref[jq], panels, preferred_element_type=jnp.float32)
        if jq < rows:
            keep_ref[jq] = total
        else:
            send_refs[jq // rows - 1][jq % rows] = total.astype(jnp.bfloat16)
    if not final:
        for d, x_ref in zip(early, x_refs):
            panels_ref[d] = x_ref[...]


def solve_kernel(level, me_ref, keep_ref, b_ref, d_ref, away_ref, *refs):
    other_refs, out_ref, piece_refs = refs[: -PAIR - 1], refs[-PAIR - 1], refs[-PAIR:]
    size, width = keep_ref.shape[1:]
    at = (2 * level - 1) * size
    for j in range(PAIR):
        total = keep_ref[j]
        for other in other_refs:
            total += other[j].astype(jnp.float32)
        right = away_ref[at : at + size, :] if j else b_ref[level, 0, 0, :, my_columns(me_ref[0], width)]
        inverse = away_ref[at + size : at + 2 * size, :size] if j else d_ref[level, 0, 0]
        resid = (right.astype(jnp.float32) - total).astype(jnp.bfloat16)
        value = jnp.dot(inverse, resid, preferred_element_type=jnp.float32).astype(jnp.bfloat16)
        out_ref[j] = value
        piece_refs[j][...] = value


def write_kernel(me_ref, full_ref, *refs):
    piece_refs, (out_ref, sems) = refs[:-2], refs[-2:]
    width = piece_refs[0].shape[1]
    copies = [pltpu.make_async_copy(full_ref, out_ref.at[0, 0, 0], sems.at[0])]
    for i, ref in enumerate(piece_refs):
        target = out_ref.at[1 + i // PAIR, 0, 0, :, my_columns(me_ref[0] ^ (i % PAIR), width)]
        copies.append(pltpu.make_async_copy(ref, target, sems.at[1 + i]))
    for copy in copies:
        copy.start()
    for copy in copies:
        copy.wait()


def last_kernel(n, me_ref, b_ref, d_ref, keep_ref, *refs):
    other_refs, (_, out_ref, buf, sem) = refs[: n - 1], refs[n - 1 :]
    me = me_ref[0]
    width = keep_ref.shape[2]
    levels = out_ref.shape[0]
    for j in range(PAIR):
        total = keep_ref[0] if j == 0 else jnp.zeros_like(keep_ref[0])
        for jq in range(1, n):
            if jq % PAIR == j:
                total += other_refs[jq - 1][0].astype(jnp.float32)
        columns = my_columns(me ^ j, width)
        resid = (b_ref[levels - 1, 0, 0, :, columns].astype(jnp.float32) - total).astype(jnp.bfloat16)
        value = jnp.dot(d_ref[levels - 1, 0, 0], resid, preferred_element_type=jnp.float32)
        buf[:, columns] = value.astype(jnp.bfloat16)
    copy = pltpu.make_async_copy(buf, out_ref.at[levels - 1, 0, 0], sem)
    copy.start()
    copy.wait()


def after(value, *others):
    return lax.optimization_barrier((value, others))[0]


class Ring:
    def __init__(self, value, cycle):
        m = len(cycle)
        self.to_next = [(cycle[i], cycle[(i + 1) % m]) for i in range(m)]
        self.to_last = [(b, a) for a, b in self.to_next]
        self.size, self.step = m, 0
        self.found = {0: value}
        self.behind = self.ahead = value

    def advance(self):
        self.step += 1
        self.behind = lax.ppermute(self.behind, "prow", self.to_next)
        self.found[self.size - self.step] = self.behind
        if self.step < self.size - self.step:
            self.ahead = lax.ppermute(self.ahead, "prow", self.to_last)
            self.found[self.step] = self.ahead


def solve_paired(cycle, b_panels, diag_inverse, l_blocks, block_cols, live_counts):
    m = lax.axis_size("prow")
    n = lax.axis_size("pcol")
    levels, _, _, size, front = b_panels.shape
    slots = l_blocks.shape[4]
    width = front // PAIR
    place = [cycle.index(p) for p in range(m)]
    my_place = sum(jnp.where(lax.axis_index("prow") == p, place[p], 0) for p in range(m))
    me = jnp.stack([lax.axis_index("pcol"), my_place]).astype(jnp.int32)

    def send(value, bits):
        return lax.ppermute(value, "pcol", [(i, i ^ bits) for i in range(n)])

    index_shape = (-(-(levels - 1) * n // 8) * 8, LANES)

    middle = levels - 1

    full, index, own, away = pl.pallas_call(
        functools.partial(first_kernel, n, m, place),
        out_shape=[
            near((size, front)),
            near(index_shape, jnp.int32),
            near((size, width)),
            near(((2 * middle - 1) * size, width)),
        ],
        in_specs=[smem()] + [anywhere()] * 4,
        out_specs=[vmem()] * 4,
        scratch_shapes=[
            pltpu.VMEM((middle, size, front), jnp.bfloat16),
            pltpu.VMEM((middle, size, size), jnp.bfloat16),
            pltpu.SMEM(live_counts.shape, jnp.int32),
            pltpu.VMEM(block_cols.shape, jnp.int32),
            pltpu.SemaphoreType.DMA((4,)),
        ],
        compiler_params=params(),
    )(me, *[in_hbm(v) for v in (live_counts, block_cols, b_panels, diag_inverse)])
    away, index = send(away, 1), [index, send(index, 1)]
    solved = after(jnp.stack([own, away[:size]]), index[1])
    blocks = [in_hbm(l_blocks), send(after(l_blocks, solved), 1)]

    late = [d for d in range(1, m) if min(d, m - d) >= m // 2 - 1]
    early = [d for d in range(m) if d not in late]
    columns, kept = [], []
    for level in range(1, levels):
        final = level == levels - 1
        ring = Ring(solved, cycle)
        for _ in range(m // 2):
            ring.advance()
        total, chosen = pl.pallas_call(
            functools.partial(gather_kernel, n, level, m, early, late),
            out_shape=[near((n, size, width), jnp.float32), near((n, size, len(late) * PAIR * size))],
            in_specs=[smem()] * (1 + PAIR) + [anywhere()] + [vmem()] * (PAIR - 1 + len(kept) + len(early)),
            out_specs=[vmem()] * 2,
            scratch_shapes=[
                pltpu.VMEM((level * m, PAIR, size, width), jnp.bfloat16),
                pltpu.VMEM(l_blocks.shape[3:], jnp.bfloat16),
                pltpu.SemaphoreType.DMA,
            ],
            compiler_params=params(),
        )(me, *index, *blocks, *kept, *[ring.found[d] for d in early])
        rows = 1 if final else PAIR
        out_shape = [near((rows, size, width), jnp.float32)] + [near((rows, size, width))] * (n // rows - 1)
        if not final:
            out_shape = [near((m, PAIR, size, width))] + out_shape
        found = pl.pallas_call(
            functools.partial(late_kernel, n, early, late, final),
            out_shape=out_shape,
            in_specs=[vmem()] * (2 + m),
            out_specs=[vmem()] * len(out_shape),
            compiler_params=params(),
        )(
            total,
            chosen,
            *[ring.found[d] for d in early + late],
        )
        if not final:
            panels, *found = found
            kept.append(panels)
        keep, *partial = found
        others = [send(v, rows * (h + 1)) for h, v in enumerate(partial)]
        if final:
            columns = [send(after(v, keep), 1) if i % PAIR else v for i, v in enumerate(columns)]
            break
        solved, *pieces = pl.pallas_call(
            functools.partial(solve_kernel, level),
            out_shape=[near((PAIR, size, width))] + [near((size, width))] * PAIR,
            in_specs=[smem()] + [vmem()] * (4 + len(others)),
            out_specs=[vmem()] * (1 + PAIR),
            compiler_params=params(),
        )(me, keep, b_panels, diag_inverse, away, *others)
        columns += pieces

    result = pl.pallas_call(
        write_kernel,
        out_shape=struct(b_panels.shape),
        in_specs=[smem()] + [vmem()] * (1 + len(columns)),
        out_specs=anywhere(),
        scratch_shapes=[pltpu.SemaphoreType.DMA((1 + len(columns),))],
        compiler_params=params(),
    )(me, full, *columns)
    return pl.pallas_call(
        functools.partial(last_kernel, n),
        out_shape=struct(b_panels.shape),
        in_specs=[smem()] + [vmem()] * (3 + len(others)) + [anywhere()],
        out_specs=anywhere(),
        scratch_shapes=[pltpu.VMEM((size, front), jnp.bfloat16), pltpu.SemaphoreType.DMA],
        input_output_aliases={4 + len(others): 0},
        compiler_params=params(),
    )(me, b_panels, diag_inverse, keep, *others, result)


def cycle_of(mesh):
    m = mesh.shape["prow"]
    names = list(mesh.axis_names)
    devices = mesh.devices.transpose([names.index("prow"), names.index("pcol")])[:, 0]
    spots = [tuple(getattr(d, "coords", None) or (i, 0, 0)) for i, d in enumerate(devices)]

    def near(a, b):
        return sum(abs(u - v) for u, v in zip(spots[a], spots[b])) == 1

    def extend(path):
        if len(path) == m:
            return path if near(path[-1], path[0]) else None
        for p in range(m):
            if p not in path and near(path[-1], p):
                found = extend(path + [p])
                if found:
                    return found
        return None

    return extend([0]) or list(range(m))


def solution(mesh):
    n = mesh.shape["pcol"]
    cycle = cycle_of(mesh)

    def shards(b_panels, diag_inverse, l_blocks, block_cols, live_counts):
        front = b_panels.shape[-1]
        rows = mesh.shape["prow"]
        paired = n & (n - 1) == 0 and n >= PAIR and rows % 2 == 0 and rows > 2 and front % (PAIR * LANES) == 0
        paired = paired and b_panels.shape[0] > 1 and front >= PAIR * b_panels.shape[-2]
        if paired and l_blocks.size * l_blocks.dtype.itemsize <= BLOCK_BYTES:
            return solve_paired(cycle, b_panels, diag_inverse, l_blocks, block_cols, live_counts)
        return solve_scattered(b_panels, diag_inverse, l_blocks, block_cols, live_counts)

    return jax.shard_map(
        shards,
        mesh=mesh,
        in_specs=(
            P(None, "prow", "pcol", None, None),
            P(None, "prow", "pcol", None, None),
            P(None, "prow", "pcol", None, None, None, None),
            P(None, "prow", "pcol", None, None),
            P(None, "prow", "pcol", None),
        ),
        out_specs=P(None, "prow", "pcol", None, None),
        check_vma=False,
    )
```

```python
import functools

import jax
import jax.numpy as jnp
from jax import lax
from jax.experimental import pallas as pl
from jax.experimental.pallas import tpu as pltpu
from jax.sharding import PartitionSpec as P

LANES = 128
PAIR = 2
BLOCK_BYTES = 4 * 2**20
VMEM_BYTES = 16 * 2**20


def vmem():
    return pl.BlockSpec(memory_space=pltpu.VMEM)


def smem():
    return pl.BlockSpec(memory_space=pltpu.SMEM)


def anywhere():
    return pl.BlockSpec(memory_space=pl.ANY)


def in_hbm(value):
    return pltpu.with_memory_space_constraint(value, pltpu.HBM)


def struct(shape, dtype=jnp.bfloat16):
    return jax.ShapeDtypeStruct(shape, dtype)


def near(shape, dtype=jnp.bfloat16):
    return pltpu.VMEM(shape, dtype)


def params():
    return pltpu.CompilerParams(vmem_limit_bytes=VMEM_BYTES)


def solve_scattered(b_panels, diag_inverse, l_blocks, block_cols, live_counts):
    proc_rows = lax.axis_size("prow")
    proc_cols = lax.axis_size("pcol")
    per_level = proc_rows * proc_cols
    right_cols = b_panels[:, 0, 0]
    levels, block_size, front_width = right_cols.shape
    slot_count = l_blocks.shape[4]
    solved_cols = jnp.zeros((levels * proc_rows, block_size, front_width), jnp.bfloat16)
    solutions = []
    for level in range(levels):
        right_part = right_cols[level].astype(jnp.float32)
        if level > 0:
            chosen = block_cols[level - 1, 0, 0]
            active = live_counts[level - 1, 0, 0]
            local_index = chosen // per_level * proc_rows + chosen % per_level // proc_cols
            live = jnp.arange(slot_count)[None, :] < active[:, None]
            masked = jnp.where(live[:, :, None, None], l_blocks[level - 1, 0, 0], jnp.zeros((), jnp.bfloat16))
            partial = jnp.einsum(
                "jkab,jkbr->jar", masked, solved_cols[local_index], preferred_element_type=jnp.float32
            ).astype(jnp.bfloat16)
            row_total = lax.psum_scatter(partial, "pcol", scatter_dimension=0, tiled=True)
            right_part = right_part - row_total[0].astype(jnp.float32)
        resid = right_part.astype(jnp.bfloat16)
        solved = jnp.dot(diag_inverse[level, 0, 0], resid, preferred_element_type=jnp.float32).astype(jnp.bfloat16)
        solutions.append(solved)
        if level + 1 < levels:
            segment = lax.all_gather(solved[None], "prow", axis=0, tiled=True)
            solved_cols = lax.dynamic_update_slice_in_dim(solved_cols, segment, level * proc_rows, 0)
    return jnp.stack(solutions)[:, None, None]


def first_kernel(n, m, place, me_ref, counts_ref, cols_ref, b_ref, d_ref, full_ref, index_ref, own_ref, away_ref, *refs):
    b_buf, d_buf, count_ref, col_ref, sems = refs
    middle = b_buf.shape[0]
    copies = [
        pltpu.make_async_copy(counts_ref, count_ref, sems.at[0]),
        pltpu.make_async_copy(cols_ref, col_ref, sems.at[1]),
        pltpu.make_async_copy(d_ref.at[pl.ds(0, middle), 0, 0], d_buf, sems.at[2]),
        pltpu.make_async_copy(b_ref.at[pl.ds(0, middle), 0, 0], b_buf, sems.at[3]),
    ]
    for copy in copies:
        copy.start()
    me, my_place = me_ref[0], me_ref[1]
    size, width = own_ref.shape
    for copy in copies[2:]:
        copy.wait()
    full_ref[...] = jnp.dot(d_buf[0], b_buf[0], preferred_element_type=jnp.float32).astype(jnp.bfloat16)
    own_ref[...] = full_ref[:, my_columns(me, width)]
    away_ref[:size, :] = full_ref[:, my_columns(me ^ 1, width)]
    for level in range(1, middle):
        at = (2 * level - 1) * size
        away_ref[at : at + size, :] = b_buf[level, :, my_columns(me ^ 1, width)]
        away_ref[at + size : at + 2 * size, :size] = d_buf[level]
        away_ref[at + size : at + 2 * size, size:] = jnp.zeros((size, width - size), jnp.bfloat16)
    for copy in copies[:2]:
        copy.wait()
    levels, slots = col_ref.shape[0] + 1, col_ref.shape[-1]
    row_at = lax.broadcasted_iota(jnp.int32, (n, slots), 0)
    slot_at = lax.broadcasted_iota(jnp.int32, (n, slots), 1)
    index_ref[...] = jnp.zeros_like(index_ref)
    for level in range(1, levels):
        rest = col_ref[level - 1, 0, 0]
        first = jnp.zeros_like(rest)
        for _ in range(1, level):
            past = rest >= m * n
            first += jnp.where(past, m, 0)
            rest -= jnp.where(past, m * n, 0)
        ahead = place[0] - my_place + jnp.zeros_like(rest)
        for p in range(1, m):
            ahead += jnp.where(rest >= p * n, place[p] - place[p - 1], 0)
        entry = first + jnp.where(ahead < 0, ahead + m, ahead)
        count = jnp.zeros_like(rest)
        for q in range(n):
            count = jnp.where(row_at == q, count_ref[level - 1, 0, 0, q], count)
        index_ref[(level - 1) * n : level * n, :slots] = jnp.where(slot_at < count, entry, -1)


def my_columns(me, width):
    return pl.ds(pl.multiple_of((me & 1) * width, LANES), width)


def gather_kernel(n, level, m, early, late, me_ref, *refs):
    index_refs, l_refs, refs = refs[:PAIR], refs[PAIR : 2 * PAIR], refs[2 * PAIR :]
    old_refs, refs = refs[: level - 1], refs[level - 1 :]
    x_refs, (total_ref, chosen_ref, known, own, sem) = refs[:-5], refs[-5:]
    copy = pltpu.make_async_copy(l_refs[0].at[level - 1, 0, 0], own, sem)
    copy.start()
    me = me_ref[0]
    size, width = total_ref.shape[1:]
    slots = l_refs[0].shape[4]
    base = (level - 1) * m
    for back in range(level - 1):
        known[back * m : (back + 1) * m] = old_refs[back][...]
    for d, x_ref in zip(early, x_refs):
        known[base + d] = x_ref[...]
    none = jnp.zeros((size, width), jnp.bfloat16)
    no_block = jnp.zeros((size, size), jnp.bfloat16)
    for j in reversed(range(PAIR)):
        if j == 0:
            copy.wait()
        for jq in range(n):
            q = me ^ jq
            blocks, solved, chosen = [], [], [no_block] * len(late)
            for k in range(slots):
                entry = index_refs[j][(level - 1) * n + q, k]
                use = entry >= 0
                block = l_refs[j][level - 1, 0, 0, q, k] if j else own[q, k]
                for i, d in enumerate(late):
                    is_late = entry == base + d
                    use = jnp.logical_and(use, entry != base + d)
                    chosen[i] = jnp.where(is_late, block, chosen[i])
                blocks.append(block)
                solved.append(jnp.where(use, known[jnp.maximum(entry, 0), j], none))
            product = jnp.dot(
                jnp.concatenate(blocks, axis=1), jnp.concatenate(solved, axis=0), preferred_element_type=jnp.float32
            )
            total_ref[jq] = product if j == PAIR - 1 else total_ref[jq] + product
            for i in range(len(late)):
                at = (i * PAIR + j) * size
                chosen_ref[jq, :, at : at + size] = chosen[i]


def late_total(jq, total_ref, chosen_ref, panels):
    return total_ref[jq] + jnp.dot(chosen_ref[jq], panels, preferred_element_type=jnp.float32)


def late_panels(x_refs):
    return jnp.concatenate([x_ref[j] for x_ref in x_refs for j in range(PAIR)], axis=0)


def away_kernel(late, total_ref, chosen_ref, *refs):
    panels, out_refs = late_panels(refs[:late]), refs[late:]
    rows = out_refs[0].shape[0]
    for i, out_ref in enumerate(out_refs):
        for row in range(rows):
            out_ref[row] = late_total(PAIR + i * rows + row, total_ref, chosen_ref, panels).astype(jnp.bfloat16)


def stay_kernel(level, late, early, me_ref, b_ref, d_ref, away_ref, total_ref, chosen_ref, *refs):
    x_refs, (right_ref, inverse_ref, panels_ref) = refs[: len(late) + len(early)], refs[len(late) + len(early) :]
    panels = late_panels(x_refs[: len(late)])
    size, width = right_ref.shape[1:]
    at = (2 * level - 1) * size
    for j in range(PAIR):
        total = late_total(j, total_ref, chosen_ref, panels)
        right = away_ref[at : at + size, :] if j else b_ref[level, 0, 0, :, my_columns(me_ref[0], width)]
        right_ref[j] = right.astype(jnp.float32) - total
        inverse_ref[j] = away_ref[at + size : at + 2 * size, :size] if j else d_ref[level, 0, 0]
    for d, x_ref in zip(late + early, x_refs):
        panels_ref[d] = x_ref[...]


def last_stay_kernel(late, me_ref, b_ref, total_ref, chosen_ref, *refs):
    x_refs, (right_ref, send_ref) = refs[:late], refs[late:]
    panels = late_panels(x_refs)
    level, width = b_ref.shape[0] - 1, right_ref.shape[2]
    send_ref[...] = late_total(1, total_ref, chosen_ref, panels).astype(jnp.bfloat16)
    for j in range(PAIR):
        right_ref[j] = b_ref[level, 0, 0, :, my_columns(me_ref[0] ^ j, width)].astype(jnp.float32)
    right_ref[0] = right_ref[0] - late_total(0, total_ref, chosen_ref, panels)


def solve_kernel(right_ref, inverse_ref, *refs):
    other_refs, out_ref = refs[:-1], refs[-1]
    for j in range(PAIR):
        resid = right_ref[j]
        for other in other_refs:
            resid -= other[j].astype(jnp.float32)
        value = jnp.dot(inverse_ref[j], resid.astype(jnp.bfloat16), preferred_element_type=jnp.float32)
        out_ref[j] = value.astype(jnp.bfloat16)


def write_kernel(me_ref, full_ref, *refs):
    level_refs, (out_ref, sems) = refs[:-2], refs[-2:]
    width = level_refs[0].shape[2]
    copies = [pltpu.make_async_copy(full_ref, out_ref.at[0, 0, 0], sems.at[0])]
    for i, ref in enumerate(level_refs):
        target = out_ref.at[1 + i // PAIR, 0, 0, :, my_columns(me_ref[0] ^ (i % PAIR), width)]
        copies.append(pltpu.make_async_copy(ref if i % PAIR else ref.at[0], target, sems.at[1 + i]))
    for copy in copies:
        copy.start()
    for copy in copies:
        copy.wait()


def last_kernel(me_ref, d_ref, right_ref, mate_ref, *refs):
    other_refs, (_, out_ref, buf, sem) = refs[:-4], refs[-4:]
    width = right_ref.shape[2]
    levels = out_ref.shape[0]
    for j in range(PAIR):
        resid = right_ref[j]
        if j:
            resid -= mate_ref[...].astype(jnp.float32)
        for other in other_refs[j::PAIR]:
            resid -= other[0].astype(jnp.float32)
        value = jnp.dot(d_ref[levels - 1, 0, 0], resid.astype(jnp.bfloat16), preferred_element_type=jnp.float32)
        buf[:, my_columns(me_ref[0] ^ j, width)] = value.astype(jnp.bfloat16)
    copy = pltpu.make_async_copy(buf, out_ref.at[levels - 1, 0, 0], sem)
    copy.start()
    copy.wait()


def after(value, *others):
    return lax.optimization_barrier((value, others))[0]


class Ring:
    def __init__(self, value, cycle):
        m = len(cycle)
        self.to_next = [(cycle[i], cycle[(i + 1) % m]) for i in range(m)]
        self.to_last = [(b, a) for a, b in self.to_next]
        self.size, self.step = m, 0
        self.found = {0: value}
        self.behind = self.ahead = value

    def advance(self):
        self.step += 1
        self.behind = lax.ppermute(self.behind, "prow", self.to_next)
        self.found[self.size - self.step] = self.behind
        if self.step < self.size - self.step:
            self.ahead = lax.ppermute(self.ahead, "prow", self.to_last)
            self.found[self.step] = self.ahead


def solve_paired(cycle, b_panels, diag_inverse, l_blocks, block_cols, live_counts):
    m = lax.axis_size("prow")
    n = lax.axis_size("pcol")
    levels, _, _, size, front = b_panels.shape
    slots = l_blocks.shape[4]
    width = front // PAIR
    place = [cycle.index(p) for p in range(m)]
    my_place = sum(jnp.where(lax.axis_index("prow") == p, place[p], 0) for p in range(m))
    me = jnp.stack([lax.axis_index("pcol"), my_place]).astype(jnp.int32)

    def send(value, bits):
        return lax.ppermute(value, "pcol", [(i, i ^ bits) for i in range(n)])

    index_shape = (-(-(levels - 1) * n // 8) * 8, LANES)

    middle = levels - 1

    full, index, own, away = pl.pallas_call(
        functools.partial(first_kernel, n, m, place),
        out_shape=[
            near((size, front)),
            near(index_shape, jnp.int32),
            near((size, width)),
            near(((2 * middle - 1) * size, width)),
        ],
        in_specs=[smem()] + [anywhere()] * 4,
        out_specs=[vmem()] * 4,
        scratch_shapes=[
            pltpu.VMEM((middle, size, front), jnp.bfloat16),
            pltpu.VMEM((middle, size, size), jnp.bfloat16),
            pltpu.SMEM(live_counts.shape, jnp.int32),
            pltpu.VMEM(block_cols.shape, jnp.int32),
            pltpu.SemaphoreType.DMA((4,)),
        ],
        compiler_params=params(),
    )(me, *[in_hbm(v) for v in (live_counts, block_cols, b_panels, diag_inverse)])
    away, index = send(away, 1), [index, send(index, 1)]
    solved = after(jnp.stack([own, away[:size]]), index[1])
    blocks = [in_hbm(l_blocks), send(after(l_blocks, solved), 1)]

    late = [d for d in range(1, m) if min(d, m - d) >= m // 2 - 1]
    early = [d for d in range(m) if d not in late]
    columns, kept = [], []
    for level in range(1, levels):
        final = level == levels - 1
        ring = Ring(solved, cycle)
        for _ in range(m // 2):
            ring.advance()
        total, chosen = pl.pallas_call(
            functools.partial(gather_kernel, n, level, m, early, late),
            out_shape=[near((n, size, width), jnp.float32), near((n, size, len(late) * PAIR * size))],
            in_specs=[smem()] * (1 + PAIR) + [anywhere()] + [vmem()] * (PAIR - 1 + len(kept) + len(early)),
            out_specs=[vmem()] * 2,
            scratch_shapes=[
                pltpu.VMEM((level * m, PAIR, size, width), jnp.bfloat16),
                pltpu.VMEM(l_blocks.shape[3:], jnp.bfloat16),
                pltpu.SemaphoreType.DMA,
            ],
            compiler_params=params(),
        )(me, *index, *blocks, *kept, *[ring.found[d] for d in early])
        rows = 1 if final else PAIR
        late_x, early_x = [ring.found[d] for d in late], [ring.found[d] for d in early]
        partial = pl.pallas_call(
            functools.partial(away_kernel, len(late)),
            out_shape=[near((rows, size, width))] * ((n - PAIR) // rows),
            in_specs=[vmem()] * (2 + len(late)),
            out_specs=[vmem()] * ((n - PAIR) // rows),
            compiler_params=params(),
        )(total, chosen, *late_x)
        others = [send(v, PAIR + rows * i) for i, v in enumerate(partial)]
        if final:
            columns = [v for solved in columns for v in (solved, send(after(solved, total)[1], 1))]
        total = after(total, partial)
        if final:
            break
        right, inverse, panels = pl.pallas_call(
            functools.partial(stay_kernel, level, late, early),
            out_shape=[
                near((PAIR, size, width), jnp.float32),
                near((PAIR, size, size)),
                near((m, PAIR, size, width)),
            ],
            in_specs=[smem()] + [vmem()] * (5 + m),
            out_specs=[vmem()] * 3,
            compiler_params=params(),
        )(me, b_panels, diag_inverse, away, total, chosen, *late_x, *early_x)
        kept.append(panels)
        solved = pl.pallas_call(
            solve_kernel,
            out_shape=near((PAIR, size, width)),
            in_specs=[vmem()] * (2 + len(others)),
            out_specs=vmem(),
            compiler_params=params(),
        )(right, inverse, *others)
        columns.append(solved)

    right, mate = pl.pallas_call(
        functools.partial(last_stay_kernel, len(late)),
        out_shape=[near((PAIR, size, width), jnp.float32), near((size, width))],
        in_specs=[smem()] + [vmem()] * (3 + len(late)),
        out_specs=[vmem()] * 2,
        compiler_params=params(),
    )(me, b_panels, total, chosen, *late_x)
    mate = send(after(mate, others[0]), 1)
    result = pl.pallas_call(
        write_kernel,
        out_shape=struct(b_panels.shape),
        in_specs=[smem()] + [vmem()] * (1 + len(columns)),
        out_specs=anywhere(),
        scratch_shapes=[pltpu.SemaphoreType.DMA((1 + len(columns),))],
        compiler_params=params(),
    )(me, full, *columns)
    return pl.pallas_call(
        last_kernel,
        out_shape=struct(b_panels.shape),
        in_specs=[smem()] + [vmem()] * (3 + len(others)) + [anywhere()],
        out_specs=anywhere(),
        scratch_shapes=[pltpu.VMEM((size, front), jnp.bfloat16), pltpu.SemaphoreType.DMA],
        input_output_aliases={4 + len(others): 0},
        compiler_params=params(),
    )(me, diag_inverse, right, mate, *others, result)


def cycle_of(mesh):
    m = mesh.shape["prow"]
    names = list(mesh.axis_names)
    devices = mesh.devices.transpose([names.index("prow"), names.index("pcol")])[:, 0]
    spots = [tuple(getattr(d, "coords", None) or (i, 0, 0)) for i, d in enumerate(devices)]

    def near(a, b):
        return sum(abs(u - v) for u, v in zip(spots[a], spots[b])) == 1

    def extend(path):
        if len(path) == m:
            return path if near(path[-1], path[0]) else None
        for p in range(m):
            if p not in path and near(path[-1], p):
                found = extend(path + [p])
                if found:
                    return found
        return None

    return extend([0]) or list(range(m))


def solution(mesh):
    n = mesh.shape["pcol"]
    cycle = cycle_of(mesh)

    def shards(b_panels, diag_inverse, l_blocks, block_cols, live_counts):
        front = b_panels.shape[-1]
        rows = mesh.shape["prow"]
        paired = n & (n - 1) == 0 and n >= PAIR and rows % 2 == 0 and rows > 2 and front % (PAIR * LANES) == 0
        paired = paired and n > PAIR and b_panels.shape[0] > 2 and front >= PAIR * b_panels.shape[-2]
        if paired and l_blocks.size * l_blocks.dtype.itemsize <= BLOCK_BYTES:
            return solve_paired(cycle, b_panels, diag_inverse, l_blocks, block_cols, live_counts)
        return solve_scattered(b_panels, diag_inverse, l_blocks, block_cols, live_counts)

    return jax.shard_map(
        shards,
        mesh=mesh,
        in_specs=(
            P(None, "prow", "pcol", None, None),
            P(None, "prow", "pcol", None, None),
            P(None, "prow", "pcol", None, None, None, None),
            P(None, "prow", "pcol", None, None),
            P(None, "prow", "pcol", None),
        ),
        out_specs=P(None, "prow", "pcol", None, None),
        check_vma=False,
    )
```

```python
import functools

import jax
import jax.numpy as jnp
from jax import lax
from jax.experimental import pallas as pl
from jax.experimental.pallas import tpu as pltpu
from jax.sharding import PartitionSpec as P

LANES = 128
PAIR = 2
BLOCK_BYTES = 4 * 2**20
VMEM_BYTES = 16 * 2**20


def vmem():
    return pl.BlockSpec(memory_space=pltpu.VMEM)


def smem():
    return pl.BlockSpec(memory_space=pltpu.SMEM)


def anywhere():
    return pl.BlockSpec(memory_space=pl.ANY)


def in_hbm(value):
    return pltpu.with_memory_space_constraint(value, pltpu.HBM)


def struct(shape, dtype=jnp.bfloat16):
    return jax.ShapeDtypeStruct(shape, dtype)


def near(shape, dtype=jnp.bfloat16):
    return pltpu.VMEM(shape, dtype)


def params():
    return pltpu.CompilerParams(vmem_limit_bytes=VMEM_BYTES)


def solve_scattered(b_panels, diag_inverse, l_blocks, block_cols, live_counts):
    proc_rows = lax.axis_size("prow")
    proc_cols = lax.axis_size("pcol")
    per_level = proc_rows * proc_cols
    right_cols = b_panels[:, 0, 0]
    levels, block_size, front_width = right_cols.shape
    slot_count = l_blocks.shape[4]
    solved_cols = jnp.zeros((levels * proc_rows, block_size, front_width), jnp.bfloat16)
    solutions = []
    for level in range(levels):
        right_part = right_cols[level].astype(jnp.float32)
        if level > 0:
            chosen = block_cols[level - 1, 0, 0]
            active = live_counts[level - 1, 0, 0]
            local_index = chosen // per_level * proc_rows + chosen % per_level // proc_cols
            live = jnp.arange(slot_count)[None, :] < active[:, None]
            masked = jnp.where(live[:, :, None, None], l_blocks[level - 1, 0, 0], jnp.zeros((), jnp.bfloat16))
            partial = jnp.einsum(
                "jkab,jkbr->jar", masked, solved_cols[local_index], preferred_element_type=jnp.float32
            ).astype(jnp.bfloat16)
            row_total = lax.psum_scatter(partial, "pcol", scatter_dimension=0, tiled=True)
            right_part = right_part - row_total[0].astype(jnp.float32)
        resid = right_part.astype(jnp.bfloat16)
        solved = jnp.dot(diag_inverse[level, 0, 0], resid, preferred_element_type=jnp.float32).astype(jnp.bfloat16)
        solutions.append(solved)
        if level + 1 < levels:
            segment = lax.all_gather(solved[None], "prow", axis=0, tiled=True)
            solved_cols = lax.dynamic_update_slice_in_dim(solved_cols, segment, level * proc_rows, 0)
    return jnp.stack(solutions)[:, None, None]


def first_kernel(n, m, place, me_ref, counts_ref, cols_ref, b_ref, d_ref, full_ref, index_ref, own_ref, other_ref, away_ref, *refs):
    b_buf, d_buf, count_ref, col_ref, sems = refs
    middle = b_buf.shape[0]
    copies = [
        pltpu.make_async_copy(counts_ref, count_ref, sems.at[0]),
        pltpu.make_async_copy(cols_ref, col_ref, sems.at[1]),
        pltpu.make_async_copy(d_ref.at[pl.ds(0, middle), 0, 0], d_buf, sems.at[2]),
        pltpu.make_async_copy(b_ref.at[pl.ds(0, middle), 0, 0], b_buf, sems.at[3]),
    ]
    for copy in copies:
        copy.start()
    me, my_place = me_ref[0], me_ref[1]
    size, width = own_ref.shape
    for copy in copies[2:]:
        copy.wait()
    full_ref[...] = jnp.dot(d_buf[0], b_buf[0], preferred_element_type=jnp.float32).astype(jnp.bfloat16)
    own_ref[...] = full_ref[:, my_columns(me, width)]
    other_ref[...] = full_ref[:, my_columns(me ^ 1, width)]
    for level in range(1, middle):
        at = (2 * level - 2) * size
        away_ref[at : at + size, :] = b_buf[level, :, my_columns(me ^ 1, width)]
        away_ref[at + size : at + 2 * size, :size] = d_buf[level]
        away_ref[at + size : at + 2 * size, size:] = jnp.zeros((size, width - size), jnp.bfloat16)
    for copy in copies[:2]:
        copy.wait()
    levels, slots = col_ref.shape[0] + 1, col_ref.shape[-1]
    row_at = lax.broadcasted_iota(jnp.int32, (n, slots), 0)
    slot_at = lax.broadcasted_iota(jnp.int32, (n, slots), 1)
    index_ref[...] = jnp.zeros_like(index_ref)
    for level in range(1, levels):
        rest = col_ref[level - 1, 0, 0]
        first = jnp.zeros_like(rest)
        for _ in range(1, level):
            past = rest >= m * n
            first += jnp.where(past, m, 0)
            rest -= jnp.where(past, m * n, 0)
        ahead = place[0] - my_place + jnp.zeros_like(rest)
        for p in range(1, m):
            ahead += jnp.where(rest >= p * n, place[p] - place[p - 1], 0)
        entry = first + jnp.where(ahead < 0, ahead + m, ahead)
        count = jnp.zeros_like(rest)
        for q in range(n):
            count = jnp.where(row_at == q, count_ref[level - 1, 0, 0, q], count)
        index_ref[(level - 1) * n : level * n, :slots] = jnp.where(slot_at < count, entry, -1)


def my_columns(me, width):
    return pl.ds(pl.multiple_of((me & 1) * width, LANES), width)


def gather_kernel(n, level, m, early, late, me_ref, *refs):
    index_refs, l_refs, refs = refs[:PAIR], refs[PAIR : 2 * PAIR], refs[2 * PAIR :]
    old_refs, refs = refs[: level - 1], refs[level - 1 :]
    x_refs, (total_ref, chosen_ref, known, own, sem) = refs[:-5], refs[-5:]
    copy = pltpu.make_async_copy(l_refs[0].at[level - 1, 0, 0], own, sem)
    copy.start()
    me = me_ref[0]
    size, width = total_ref.shape[1:]
    slots = l_refs[0].shape[4]
    base = (level - 1) * m
    for back in range(level - 1):
        known[back * m : (back + 1) * m] = old_refs[back][...]
    for d, x_ref in zip(early, x_refs):
        known[base + d] = x_ref[...]
    none = jnp.zeros((size, width), jnp.bfloat16)
    no_block = jnp.zeros((size, size), jnp.bfloat16)
    for j in reversed(range(PAIR)):
        if j == 0:
            copy.wait()
        for jq in range(n):
            q = me ^ jq
            blocks, solved, chosen = [], [], [no_block] * len(late)
            for k in range(slots):
                entry = index_refs[j][(level - 1) * n + q, k]
                use = entry >= 0
                block = l_refs[j][level - 1, 0, 0, q, k] if j else own[q, k]
                for i, d in enumerate(late):
                    is_late = entry == base + d
                    use = jnp.logical_and(use, entry != base + d)
                    chosen[i] = jnp.where(is_late, block, chosen[i])
                blocks.append(block)
                solved.append(jnp.where(use, known[jnp.maximum(entry, 0), j], none))
            product = jnp.dot(
                jnp.concatenate(blocks, axis=1), jnp.concatenate(solved, axis=0), preferred_element_type=jnp.float32
            )
            total_ref[jq] = product if j == PAIR - 1 else total_ref[jq] + product
            for i in range(len(late)):
                at = (i * PAIR + j) * size
                chosen_ref[jq, :, at : at + size] = chosen[i]


def late_total(jq, total_ref, chosen_ref, panels):
    return total_ref[jq] + jnp.dot(chosen_ref[jq], panels, preferred_element_type=jnp.float32)


def late_panels(x_refs):
    return jnp.concatenate([x_ref[j] for x_ref in x_refs for j in range(PAIR)], axis=0)


def away_kernel(late, total_ref, chosen_ref, *refs):
    panels, out_refs = late_panels(refs[:late]), refs[late:]
    rows = out_refs[0].shape[0]
    for i, out_ref in enumerate(out_refs):
        for row in range(rows):
            out_ref[row] = late_total(PAIR + i * rows + row, total_ref, chosen_ref, panels).astype(jnp.bfloat16)


def stay_kernel(level, late, early, me_ref, b_ref, d_ref, away_ref, total_ref, chosen_ref, *refs):
    x_refs, (right_ref, inverse_ref, panels_ref) = refs[: len(late) + len(early)], refs[len(late) + len(early) :]
    panels = late_panels(x_refs[: len(late)])
    size, width = right_ref.shape[1:]
    at = (2 * level - 2) * size
    for j in range(PAIR):
        total = late_total(j, total_ref, chosen_ref, panels)
        right = away_ref[at : at + size, :] if j else b_ref[level, 0, 0, :, my_columns(me_ref[0], width)]
        right_ref[j] = right.astype(jnp.float32) - total
        inverse_ref[j] = away_ref[at + size : at + 2 * size, :size] if j else d_ref[level, 0, 0]
    for d, x_ref in zip(late + early, x_refs):
        panels_ref[d] = x_ref[...]


def last_stay_kernel(late, me_ref, b_ref, total_ref, chosen_ref, *refs):
    x_refs, (right_ref, send_ref) = refs[:late], refs[late:]
    panels = late_panels(x_refs)
    level, width = b_ref.shape[0] - 1, right_ref.shape[2]
    send_ref[...] = late_total(1, total_ref, chosen_ref, panels).astype(jnp.bfloat16)
    for j in range(PAIR):
        right_ref[j] = b_ref[level, 0, 0, :, my_columns(me_ref[0] ^ j, width)].astype(jnp.float32)
    right_ref[0] = right_ref[0] - late_total(0, total_ref, chosen_ref, panels)


def solve_kernel(right_ref, inverse_ref, *refs):
    other_refs, out_ref = refs[:-1], refs[-1]
    for j in range(PAIR):
        resid = right_ref[j]
        for other in other_refs:
            resid -= other[j].astype(jnp.float32)
        value = jnp.dot(inverse_ref[j], resid.astype(jnp.bfloat16), preferred_element_type=jnp.float32)
        out_ref[j] = value.astype(jnp.bfloat16)


def write_kernel(me_ref, full_ref, *refs):
    level_refs, (out_ref, sems) = refs[:-2], refs[-2:]
    width = level_refs[0].shape[2]
    copies = [pltpu.make_async_copy(full_ref, out_ref.at[0, 0, 0], sems.at[0])]
    for i, ref in enumerate(level_refs):
        target = out_ref.at[1 + i // PAIR, 0, 0, :, my_columns(me_ref[0] ^ (i % PAIR), width)]
        copies.append(pltpu.make_async_copy(ref if i % PAIR else ref.at[0], target, sems.at[1 + i]))
    for copy in copies:
        copy.start()
    for copy in copies:
        copy.wait()


def last_kernel(me_ref, d_ref, right_ref, mate_ref, *refs):
    other_refs, (_, out_ref, buf, sem) = refs[:-4], refs[-4:]
    width = right_ref.shape[2]
    levels = out_ref.shape[0]
    for j in range(PAIR):
        resid = right_ref[j]
        if j:
            resid -= mate_ref[...].astype(jnp.float32)
        for other in other_refs[j::PAIR]:
            resid -= other[0].astype(jnp.float32)
        value = jnp.dot(d_ref[levels - 1, 0, 0], resid.astype(jnp.bfloat16), preferred_element_type=jnp.float32)
        buf[:, my_columns(me_ref[0] ^ j, width)] = value.astype(jnp.bfloat16)
    copy = pltpu.make_async_copy(buf, out_ref.at[levels - 1, 0, 0], sem)
    copy.start()
    copy.wait()


def after(value, *others):
    return lax.optimization_barrier((value, others))[0]


class Ring:
    def __init__(self, value, cycle):
        m = len(cycle)
        self.to_next = [(cycle[i], cycle[(i + 1) % m]) for i in range(m)]
        self.to_last = [(b, a) for a, b in self.to_next]
        self.size, self.step = m, 0
        self.found = {0: value}
        self.behind = self.ahead = value

    def advance(self):
        self.step += 1
        self.behind = lax.ppermute(self.behind, "prow", self.to_next)
        self.found[self.size - self.step] = self.behind
        if self.step < self.size - self.step:
            self.ahead = lax.ppermute(self.ahead, "prow", self.to_last)
            self.found[self.step] = self.ahead


def solve_paired(cycle, b_panels, diag_inverse, l_blocks, block_cols, live_counts):
    m = lax.axis_size("prow")
    n = lax.axis_size("pcol")
    levels, _, _, size, front = b_panels.shape
    slots = l_blocks.shape[4]
    width = front // PAIR
    place = [cycle.index(p) for p in range(m)]
    my_place = sum(jnp.where(lax.axis_index("prow") == p, place[p], 0) for p in range(m))
    me = jnp.stack([lax.axis_index("pcol"), my_place]).astype(jnp.int32)

    def send(value, bits):
        return lax.ppermute(value, "pcol", [(i, i ^ bits) for i in range(n)])

    index_shape = (-(-(levels - 1) * n // 8) * 8, LANES)

    middle = levels - 1

    full, index, own, other, away = pl.pallas_call(
        functools.partial(first_kernel, n, m, place),
        out_shape=[
            near((size, front)),
            near(index_shape, jnp.int32),
            near((size, width)),
            near((size, width)),
            near(((2 * middle - 2) * size, width)),
        ],
        in_specs=[smem()] + [anywhere()] * 4,
        out_specs=[vmem()] * 5,
        scratch_shapes=[
            pltpu.VMEM((middle, size, front), jnp.bfloat16),
            pltpu.VMEM((middle, size, size), jnp.bfloat16),
            pltpu.SMEM(live_counts.shape, jnp.int32),
            pltpu.VMEM(block_cols.shape, jnp.int32),
            pltpu.SemaphoreType.DMA((4,)),
        ],
        compiler_params=params(),
    )(me, *[in_hbm(v) for v in (live_counts, block_cols, b_panels, diag_inverse)])
    other, away, index = send(other, 1), send(away, 1), [index, send(index, 1)]
    solved = after(jnp.stack([own, other]), index[1])
    blocks = [in_hbm(l_blocks), send(after(l_blocks, solved), 1)]

    late = [d for d in range(1, m) if min(d, m - d) >= m // 2 - 1]
    early = [d for d in range(m) if d not in late]
    columns, kept = [], []
    for level in range(1, levels):
        final = level == levels - 1
        ring = Ring(solved, cycle)
        for step in range(m // 2):
            if level == 1 and step == 2:
                ring.ahead = after(ring.ahead, away)
            ring.advance()
        total, chosen = pl.pallas_call(
            functools.partial(gather_kernel, n, level, m, early, late),
            out_shape=[near((n, size, width), jnp.float32), near((n, size, len(late) * PAIR * size))],
            in_specs=[smem()] * (1 + PAIR) + [anywhere()] + [vmem()] * (PAIR - 1 + len(kept) + len(early)),
            out_specs=[vmem()] * 2,
            scratch_shapes=[
                pltpu.VMEM((level * m, PAIR, size, width), jnp.bfloat16),
                pltpu.VMEM(l_blocks.shape[3:], jnp.bfloat16),
                pltpu.SemaphoreType.DMA,
            ],
            compiler_params=params(),
        )(me, *index, *blocks, *kept, *[ring.found[d] for d in early])
        rows = 1 if final else PAIR
        late_x, early_x = [ring.found[d] for d in late], [ring.found[d] for d in early]
        partial = pl.pallas_call(
            functools.partial(away_kernel, len(late)),
            out_shape=[near((rows, size, width))] * ((n - PAIR) // rows),
            in_specs=[vmem()] * (2 + len(late)),
            out_specs=[vmem()] * ((n - PAIR) // rows),
            compiler_params=params(),
        )(total, chosen, *late_x)
        others = [send(v, PAIR + rows * i) for i, v in enumerate(partial)]
        if final:
            columns = [v for solved in columns for v in (solved, send(after(solved, total)[1], 1))]
        total = after(total, partial)
        if final:
            break
        right, inverse, panels = pl.pallas_call(
            functools.partial(stay_kernel, level, late, early),
            out_shape=[
                near((PAIR, size, width), jnp.float32),
                near((PAIR, size, size)),
                near((m, PAIR, size, width)),
            ],
            in_specs=[smem()] + [vmem()] * (5 + m),
            out_specs=[vmem()] * 3,
            compiler_params=params(),
        )(me, b_panels, diag_inverse, away, total, chosen, *late_x, *early_x)
        kept.append(panels)
        solved = pl.pallas_call(
            solve_kernel,
            out_shape=near((PAIR, size, width)),
            in_specs=[vmem()] * (2 + len(others)),
            out_specs=vmem(),
            compiler_params=params(),
        )(right, inverse, *others)
        columns.append(solved)

    right, mate = pl.pallas_call(
        functools.partial(last_stay_kernel, len(late)),
        out_shape=[near((PAIR, size, width), jnp.float32), near((size, width))],
        in_specs=[smem()] + [vmem()] * (3 + len(late)),
        out_specs=[vmem()] * 2,
        compiler_params=params(),
    )(me, b_panels, total, chosen, *late_x)
    mate = send(after(mate, others[0]), 1)
    result = pl.pallas_call(
        write_kernel,
        out_shape=struct(b_panels.shape),
        in_specs=[smem()] + [vmem()] * (1 + len(columns)),
        out_specs=anywhere(),
        scratch_shapes=[pltpu.SemaphoreType.DMA((1 + len(columns),))],
        compiler_params=params(),
    )(me, full, *columns)
    return pl.pallas_call(
        last_kernel,
        out_shape=struct(b_panels.shape),
        in_specs=[smem()] + [vmem()] * (3 + len(others)) + [anywhere()],
        out_specs=anywhere(),
        scratch_shapes=[pltpu.VMEM((size, front), jnp.bfloat16), pltpu.SemaphoreType.DMA],
        input_output_aliases={4 + len(others): 0},
        compiler_params=params(),
    )(me, diag_inverse, right, mate, *others, result)


def cycle_of(mesh):
    m = mesh.shape["prow"]
    names = list(mesh.axis_names)
    devices = mesh.devices.transpose([names.index("prow"), names.index("pcol")])[:, 0]
    spots = [tuple(getattr(d, "coords", None) or (i, 0, 0)) for i, d in enumerate(devices)]

    def near(a, b):
        return sum(abs(u - v) for u, v in zip(spots[a], spots[b])) == 1

    def extend(path):
        if len(path) == m:
            return path if near(path[-1], path[0]) else None
        for p in range(m):
            if p not in path and near(path[-1], p):
                found = extend(path + [p])
                if found:
                    return found
        return None

    return extend([0]) or list(range(m))


def solution(mesh):
    n = mesh.shape["pcol"]
    cycle = cycle_of(mesh)

    def shards(b_panels, diag_inverse, l_blocks, block_cols, live_counts):
        front = b_panels.shape[-1]
        rows = mesh.shape["prow"]
        paired = n & (n - 1) == 0 and n >= PAIR and rows % 2 == 0 and rows > 2 and front % (PAIR * LANES) == 0
        paired = paired and n > PAIR and b_panels.shape[0] > 2 and front >= PAIR * b_panels.shape[-2]
        if paired and l_blocks.size * l_blocks.dtype.itemsize <= BLOCK_BYTES:
            return solve_paired(cycle, b_panels, diag_inverse, l_blocks, block_cols, live_counts)
        return solve_scattered(b_panels, diag_inverse, l_blocks, block_cols, live_counts)

    return jax.shard_map(
        shards,
        mesh=mesh,
        in_specs=(
            P(None, "prow", "pcol", None, None),
            P(None, "prow", "pcol", None, None),
            P(None, "prow", "pcol", None, None, None, None),
            P(None, "prow", "pcol", None, None),
            P(None, "prow", "pcol", None),
        ),
        out_specs=P(None, "prow", "pcol", None, None),
        check_vma=False,
    )
```

```python
import functools

import jax
import jax.numpy as jnp
from jax import lax
from jax.experimental import pallas as pl
from jax.experimental.pallas import tpu as pltpu
from jax.sharding import PartitionSpec as P

LANES = 128
PAIR = 2
BLOCK_BYTES = 4 * 2**20
VMEM_BYTES = 16 * 2**20


def vmem():
    return pl.BlockSpec(memory_space=pltpu.VMEM)


def smem():
    return pl.BlockSpec(memory_space=pltpu.SMEM)


def anywhere():
    return pl.BlockSpec(memory_space=pl.ANY)


def in_hbm(value):
    return pltpu.with_memory_space_constraint(value, pltpu.HBM)


def struct(shape, dtype=jnp.bfloat16):
    return jax.ShapeDtypeStruct(shape, dtype)


def near(shape, dtype=jnp.bfloat16):
    return pltpu.VMEM(shape, dtype)


def params():
    return pltpu.CompilerParams(vmem_limit_bytes=VMEM_BYTES)


def solve_scattered(b_panels, diag_inverse, l_blocks, block_cols, live_counts):
    proc_rows = lax.axis_size("prow")
    proc_cols = lax.axis_size("pcol")
    per_level = proc_rows * proc_cols
    right_cols = b_panels[:, 0, 0]
    levels, block_size, front_width = right_cols.shape
    slot_count = l_blocks.shape[4]
    solved_cols = jnp.zeros((levels * proc_rows, block_size, front_width), jnp.bfloat16)
    solutions = []
    for level in range(levels):
        right_part = right_cols[level].astype(jnp.float32)
        if level > 0:
            chosen = block_cols[level - 1, 0, 0]
            active = live_counts[level - 1, 0, 0]
            local_index = chosen // per_level * proc_rows + chosen % per_level // proc_cols
            live = jnp.arange(slot_count)[None, :] < active[:, None]
            masked = jnp.where(live[:, :, None, None], l_blocks[level - 1, 0, 0], jnp.zeros((), jnp.bfloat16))
            partial = jnp.einsum(
                "jkab,jkbr->jar", masked, solved_cols[local_index], preferred_element_type=jnp.float32
            ).astype(jnp.bfloat16)
            row_total = lax.psum_scatter(partial, "pcol", scatter_dimension=0, tiled=True)
            right_part = right_part - row_total[0].astype(jnp.float32)
        resid = right_part.astype(jnp.bfloat16)
        solved = jnp.dot(diag_inverse[level, 0, 0], resid, preferred_element_type=jnp.float32).astype(jnp.bfloat16)
        solutions.append(solved)
        if level + 1 < levels:
            segment = lax.all_gather(solved[None], "prow", axis=0, tiled=True)
            solved_cols = lax.dynamic_update_slice_in_dim(solved_cols, segment, level * proc_rows, 0)
    return jnp.stack(solutions)[:, None, None]


def first_kernel(n, m, place, counts_ref, cols_ref, b_ref, d_ref, full_ref, index_ref, own_ref, other_ref, away_ref, *refs):
    b_buf, d_buf, count_ref, col_ref, sems = refs
    middle = b_buf.shape[0]
    copies = [
        pltpu.make_async_copy(b_ref.at[0, 0, 0], b_buf.at[0], sems.at[0]),
        pltpu.make_async_copy(d_ref.at[0, 0, 0], d_buf.at[0], sems.at[1]),
        pltpu.make_async_copy(cols_ref, col_ref, sems.at[2]),
        pltpu.make_async_copy(counts_ref, count_ref, sems.at[3]),
        pltpu.make_async_copy(d_ref.at[pl.ds(1, middle - 1), 0, 0], d_buf.at[pl.ds(1, middle - 1)], sems.at[4]),
        pltpu.make_async_copy(b_ref.at[pl.ds(1, middle - 1), 0, 0], b_buf.at[pl.ds(1, middle - 1)], sems.at[5]),
    ]
    for copy in copies:
        copy.start()
    me, my_row, my_place = lax.axis_index("pcol"), lax.axis_index("prow"), place[0]
    for p in range(1, m):
        my_place = jnp.where(my_row == p, place[p], my_place)
    size, width = own_ref.shape
    for copy in copies[:2]:
        copy.wait()
    full_ref[...] = jnp.dot(d_buf[0], b_buf[0], preferred_element_type=jnp.float32).astype(jnp.bfloat16)
    own_ref[...] = full_ref[:, my_columns(me, width)]
    other_ref[...] = full_ref[:, my_columns(me ^ 1, width)]
    for copy in copies[2:]:
        copy.wait()
    for level in range(1, middle):
        at = (2 * level - 2) * size
        away_ref[at : at + size, :] = b_buf[level, :, my_columns(me ^ 1, width)]
        away_ref[at + size : at + 2 * size, :size] = d_buf[level]
        away_ref[at + size : at + 2 * size, size:] = jnp.zeros((size, width - size), jnp.bfloat16)
    levels, slots = col_ref.shape[0] + 1, col_ref.shape[-1]
    row_at = lax.broadcasted_iota(jnp.int32, (n, slots), 0)
    slot_at = lax.broadcasted_iota(jnp.int32, (n, slots), 1)
    index_ref[...] = jnp.zeros_like(index_ref)
    for level in range(1, levels):
        rest = col_ref[level - 1, 0, 0]
        first = jnp.zeros_like(rest)
        for _ in range(1, level):
            past = rest >= m * n
            first += jnp.where(past, m, 0)
            rest -= jnp.where(past, m * n, 0)
        ahead = place[0] - my_place + jnp.zeros_like(rest)
        for p in range(1, m):
            ahead += jnp.where(rest >= p * n, place[p] - place[p - 1], 0)
        entry = first + jnp.where(ahead < 0, ahead + m, ahead)
        count = jnp.zeros_like(rest)
        for q in range(n):
            count = jnp.where(row_at == q, count_ref[level - 1, 0, 0, q], count)
        index_ref[(level - 1) * n : level * n, :slots] = jnp.where(slot_at < count, entry, -1)


def my_columns(me, width):
    return pl.ds(pl.multiple_of((me & 1) * width, LANES), width)


def gather_kernel(n, level, m, early, late, *refs):
    index_refs, l_refs, refs = refs[:PAIR], refs[PAIR : 2 * PAIR], refs[2 * PAIR :]
    old_refs, refs = refs[: level - 1], refs[level - 1 :]
    x_refs, (total_ref, chosen_ref, known, own, sem) = refs[:-5], refs[-5:]
    copy = pltpu.make_async_copy(l_refs[0].at[level - 1, 0, 0], own, sem)
    copy.start()
    me = lax.axis_index("pcol")
    size, width = total_ref.shape[1:]
    slots = l_refs[0].shape[4]
    base = (level - 1) * m
    for back in range(level - 1):
        known[back * m : (back + 1) * m] = old_refs[back][...]
    for d, x_ref in zip(early, x_refs):
        known[base + d] = x_ref[...]
    none = jnp.zeros((size, width), jnp.bfloat16)
    no_block = jnp.zeros((size, size), jnp.bfloat16)
    for j in reversed(range(PAIR)):
        if j == 0:
            copy.wait()
        for jq in range(n):
            q = me ^ jq
            blocks, solved, chosen = [], [], [no_block] * len(late)
            for k in range(slots):
                entry = index_refs[j][(level - 1) * n + q, k]
                use = entry >= 0
                block = l_refs[j][level - 1, 0, 0, q, k] if j else own[q, k]
                for i, d in enumerate(late):
                    is_late = entry == base + d
                    use = jnp.logical_and(use, entry != base + d)
                    chosen[i] = jnp.where(is_late, block, chosen[i])
                blocks.append(block)
                solved.append(jnp.where(use, known[jnp.maximum(entry, 0), j], none))
            product = jnp.dot(
                jnp.concatenate(blocks, axis=1), jnp.concatenate(solved, axis=0), preferred_element_type=jnp.float32
            )
            total_ref[jq] = product if j == PAIR - 1 else total_ref[jq] + product
            for i in range(len(late)):
                at = (i * PAIR + j) * size
                chosen_ref[jq, :, at : at + size] = chosen[i]


def late_total(jq, total_ref, chosen_ref, panels):
    return total_ref[jq] + jnp.dot(chosen_ref[jq], panels, preferred_element_type=jnp.float32)


def late_panels(x_refs):
    return jnp.concatenate([x_ref[j] for x_ref in x_refs for j in range(PAIR)], axis=0)


def away_kernel(late, total_ref, chosen_ref, *refs):
    panels, out_refs = late_panels(refs[:late]), refs[late:]
    rows = out_refs[0].shape[0]
    for i, out_ref in enumerate(out_refs):
        for row in range(rows):
            out_ref[row] = late_total(PAIR + i * rows + row, total_ref, chosen_ref, panels).astype(jnp.bfloat16)


def stay_kernel(level, late, early, b_ref, d_ref, away_ref, total_ref, chosen_ref, *refs):
    x_refs, (right_ref, inverse_ref, panels_ref) = refs[: len(late) + len(early)], refs[len(late) + len(early) :]
    panels = late_panels(x_refs[: len(late)])
    size, width = right_ref.shape[1:]
    at = (2 * level - 2) * size
    for j in range(PAIR):
        total = late_total(j, total_ref, chosen_ref, panels)
        right = away_ref[at : at + size, :] if j else b_ref[level, 0, 0, :, my_columns(lax.axis_index("pcol"), width)]
        right_ref[j] = right.astype(jnp.float32) - total
        inverse_ref[j] = away_ref[at + size : at + 2 * size, :size] if j else d_ref[level, 0, 0]
    for d, x_ref in zip(late + early, x_refs):
        panels_ref[d] = x_ref[...]


def last_stay_kernel(late, b_ref, total_ref, chosen_ref, *refs):
    x_refs, (right_ref, send_ref) = refs[:late], refs[late:]
    panels = late_panels(x_refs)
    level, width = b_ref.shape[0] - 1, right_ref.shape[2]
    send_ref[...] = late_total(1, total_ref, chosen_ref, panels).astype(jnp.bfloat16)
    for j in range(PAIR):
        right_ref[j] = b_ref[level, 0, 0, :, my_columns(lax.axis_index("pcol") ^ j, width)].astype(jnp.float32)
    right_ref[0] = right_ref[0] - late_total(0, total_ref, chosen_ref, panels)


def solve_kernel(right_ref, inverse_ref, *refs):
    other_refs, out_ref = refs[:-1], refs[-1]
    for j in range(PAIR):
        resid = right_ref[j]
        for other in other_refs:
            resid -= other[j].astype(jnp.float32)
        value = jnp.dot(inverse_ref[j], resid.astype(jnp.bfloat16), preferred_element_type=jnp.float32)
        out_ref[j] = value.astype(jnp.bfloat16)


def write_kernel(full_ref, *refs):
    level_refs, (out_ref, sems) = refs[:-2], refs[-2:]
    width = level_refs[0].shape[2]
    copies = [pltpu.make_async_copy(full_ref, out_ref.at[0, 0, 0], sems.at[0])]
    for i, ref in enumerate(level_refs):
        target = out_ref.at[1 + i // PAIR, 0, 0, :, my_columns(lax.axis_index("pcol") ^ (i % PAIR), width)]
        copies.append(pltpu.make_async_copy(ref if i % PAIR else ref.at[0], target, sems.at[1 + i]))
    for copy in copies:
        copy.start()
    for copy in copies:
        copy.wait()


def last_kernel(d_ref, right_ref, mate_ref, *refs):
    other_refs, (_, out_ref, buf, sem) = refs[:-4], refs[-4:]
    width = right_ref.shape[2]
    levels = out_ref.shape[0]
    for j in range(PAIR):
        resid = right_ref[j]
        if j:
            resid -= mate_ref[...].astype(jnp.float32)
        for other in other_refs[j::PAIR]:
            resid -= other[0].astype(jnp.float32)
        value = jnp.dot(d_ref[levels - 1, 0, 0], resid.astype(jnp.bfloat16), preferred_element_type=jnp.float32)
        buf[:, my_columns(lax.axis_index("pcol") ^ j, width)] = value.astype(jnp.bfloat16)
    copy = pltpu.make_async_copy(buf, out_ref.at[levels - 1, 0, 0], sem)
    copy.start()
    copy.wait()


def after(value, *others):
    return lax.optimization_barrier((value, others))[0]


class Ring:
    def __init__(self, value, cycle):
        m = len(cycle)
        self.to_next = [(cycle[i], cycle[(i + 1) % m]) for i in range(m)]
        self.to_last = [(b, a) for a, b in self.to_next]
        self.size, self.step = m, 0
        self.found = {0: value}
        self.behind = self.ahead = value

    def advance(self):
        self.step += 1
        self.behind = lax.ppermute(self.behind, "prow", self.to_next)
        self.found[self.size - self.step] = self.behind
        if self.step < self.size - self.step:
            self.ahead = lax.ppermute(self.ahead, "prow", self.to_last)
            self.found[self.step] = self.ahead


def solve_paired(cycle, b_panels, diag_inverse, l_blocks, block_cols, live_counts):
    m = lax.axis_size("prow")
    n = lax.axis_size("pcol")
    levels, _, _, size, front = b_panels.shape
    slots = l_blocks.shape[4]
    width = front // PAIR
    place = [cycle.index(p) for p in range(m)]

    def send(value, bits):
        return lax.ppermute(value, "pcol", [(i, i ^ bits) for i in range(n)])

    index_shape = (-(-(levels - 1) * n // 8) * 8, LANES)

    middle = levels - 1

    full, index, own, other, away = pl.pallas_call(
        functools.partial(first_kernel, n, m, place),
        out_shape=[
            near((size, front)),
            near(index_shape, jnp.int32),
            near((size, width)),
            near((size, width)),
            near(((2 * middle - 2) * size, width)),
        ],
        in_specs=[anywhere()] * 4,
        out_specs=[vmem()] * 5,
        scratch_shapes=[
            pltpu.VMEM((middle, size, front), jnp.bfloat16),
            pltpu.VMEM((middle, size, size), jnp.bfloat16),
            pltpu.SMEM(live_counts.shape, jnp.int32),
            pltpu.VMEM(block_cols.shape, jnp.int32),
            pltpu.SemaphoreType.DMA((6,)),
        ],
        compiler_params=params(),
    )(*[in_hbm(v) for v in (live_counts, block_cols, b_panels, diag_inverse)])
    other, away, index = send(other, 1), send(away, 1), [index, send(index, 1)]
    solved = after(jnp.stack([own, other]), index[1])
    blocks = [in_hbm(l_blocks), send(after(l_blocks, solved), 1)]

    late = [d for d in range(1, m) if min(d, m - d) >= m // 2 - 1]
    early = [d for d in range(m) if d not in late]
    columns, kept = [], []
    for level in range(1, levels):
        final = level == levels - 1
        ring = Ring(solved, cycle)
        for step in range(m // 2):
            if level == 1 and step == 2:
                ring.ahead = after(ring.ahead, away)
            ring.advance()
        total, chosen = pl.pallas_call(
            functools.partial(gather_kernel, n, level, m, early, late),
            out_shape=[near((n, size, width), jnp.float32), near((n, size, len(late) * PAIR * size))],
            in_specs=[smem()] * PAIR + [anywhere()] + [vmem()] * (PAIR - 1 + len(kept) + len(early)),
            out_specs=[vmem()] * 2,
            scratch_shapes=[
                pltpu.VMEM((level * m, PAIR, size, width), jnp.bfloat16),
                pltpu.VMEM(l_blocks.shape[3:], jnp.bfloat16),
                pltpu.SemaphoreType.DMA,
            ],
            compiler_params=params(),
        )(*index, *blocks, *kept, *[ring.found[d] for d in early])
        rows = 1 if final else PAIR
        late_x, early_x = [ring.found[d] for d in late], [ring.found[d] for d in early]
        partial = pl.pallas_call(
            functools.partial(away_kernel, len(late)),
            out_shape=[near((rows, size, width))] * ((n - PAIR) // rows),
            in_specs=[vmem()] * (2 + len(late)),
            out_specs=[vmem()] * ((n - PAIR) // rows),
            compiler_params=params(),
        )(total, chosen, *late_x)
        others = [send(v, PAIR + rows * i) for i, v in enumerate(partial)]
        if final:
            columns = [v for solved in columns for v in (solved, send(after(solved, total)[1], 1))]
        total = after(total, partial)
        if final:
            break
        right, inverse, panels = pl.pallas_call(
            functools.partial(stay_kernel, level, late, early),
            out_shape=[
                near((PAIR, size, width), jnp.float32),
                near((PAIR, size, size)),
                near((m, PAIR, size, width)),
            ],
            in_specs=[vmem()] * (5 + m),
            out_specs=[vmem()] * 3,
            compiler_params=params(),
        )(b_panels, diag_inverse, away, total, chosen, *late_x, *early_x)
        kept.append(panels)
        solved = pl.pallas_call(
            solve_kernel,
            out_shape=near((PAIR, size, width)),
            in_specs=[vmem()] * (2 + len(others)),
            out_specs=vmem(),
            compiler_params=params(),
        )(right, inverse, *others)
        columns.append(solved)

    right, mate = pl.pallas_call(
        functools.partial(last_stay_kernel, len(late)),
        out_shape=[near((PAIR, size, width), jnp.float32), near((size, width))],
        in_specs=[vmem()] * (3 + len(late)),
        out_specs=[vmem()] * 2,
        compiler_params=params(),
    )(b_panels, total, chosen, *late_x)
    mate = send(after(mate, others[0]), 1)
    result = pl.pallas_call(
        write_kernel,
        out_shape=struct(b_panels.shape),
        in_specs=[vmem()] * (1 + len(columns)),
        out_specs=anywhere(),
        scratch_shapes=[pltpu.SemaphoreType.DMA((1 + len(columns),))],
        compiler_params=params(),
    )(full, *columns)
    return pl.pallas_call(
        last_kernel,
        out_shape=struct(b_panels.shape),
        in_specs=[vmem()] * (3 + len(others)) + [anywhere()],
        out_specs=anywhere(),
        scratch_shapes=[pltpu.VMEM((size, front), jnp.bfloat16), pltpu.SemaphoreType.DMA],
        input_output_aliases={3 + len(others): 0},
        compiler_params=params(),
    )(diag_inverse, right, mate, *others, result)


def cycle_of(mesh):
    m = mesh.shape["prow"]
    names = list(mesh.axis_names)
    devices = mesh.devices.transpose([names.index("prow"), names.index("pcol")])[:, 0]
    spots = [tuple(getattr(d, "coords", None) or (i, 0, 0)) for i, d in enumerate(devices)]

    def near(a, b):
        return sum(abs(u - v) for u, v in zip(spots[a], spots[b])) == 1

    def extend(path):
        if len(path) == m:
            return path if near(path[-1], path[0]) else None
        for p in range(m):
            if p not in path and near(path[-1], p):
                found = extend(path + [p])
                if found:
                    return found
        return None

    return extend([0]) or list(range(m))


def solution(mesh):
    n = mesh.shape["pcol"]
    cycle = cycle_of(mesh)

    def shards(b_panels, diag_inverse, l_blocks, block_cols, live_counts):
        front = b_panels.shape[-1]
        rows = mesh.shape["prow"]
        paired = n & (n - 1) == 0 and n >= PAIR and rows % 2 == 0 and rows > 2 and front % (PAIR * LANES) == 0
        paired = paired and n > PAIR and b_panels.shape[0] > 2 and front >= PAIR * b_panels.shape[-2]
        if paired and l_blocks.size * l_blocks.dtype.itemsize <= BLOCK_BYTES:
            return solve_paired(cycle, b_panels, diag_inverse, l_blocks, block_cols, live_counts)
        return solve_scattered(b_panels, diag_inverse, l_blocks, block_cols, live_counts)

    return jax.shard_map(
        shards,
        mesh=mesh,
        in_specs=(
            P(None, "prow", "pcol", None, None),
            P(None, "prow", "pcol", None, None),
            P(None, "prow", "pcol", None, None, None, None),
            P(None, "prow", "pcol", None, None),
            P(None, "prow", "pcol", None),
        ),
        out_specs=P(None, "prow", "pcol", None, None),
        check_vma=False,
    )
```

```python
import functools

import jax
import jax.numpy as jnp
from jax import lax
from jax.experimental import pallas as pl
from jax.experimental.pallas import tpu as pltpu
from jax.sharding import PartitionSpec as P

LANES = 128
PAIR = 2
BLOCK_BYTES = 4 * 2**20
VMEM_BYTES = 16 * 2**20


def vmem():
    return pl.BlockSpec(memory_space=pltpu.VMEM)


def smem():
    return pl.BlockSpec(memory_space=pltpu.SMEM)


def anywhere():
    return pl.BlockSpec(memory_space=pl.ANY)


def in_hbm(value):
    return pltpu.with_memory_space_constraint(value, pltpu.HBM)


def struct(shape, dtype=jnp.bfloat16):
    return jax.ShapeDtypeStruct(shape, dtype)


def near(shape, dtype=jnp.bfloat16):
    return pltpu.VMEM(shape, dtype)


def params():
    return pltpu.CompilerParams(vmem_limit_bytes=VMEM_BYTES)


def solve_scattered(b_panels, diag_inverse, l_blocks, block_cols, live_counts):
    proc_rows = lax.axis_size("prow")
    proc_cols = lax.axis_size("pcol")
    per_level = proc_rows * proc_cols
    right_cols = b_panels[:, 0, 0]
    levels, block_size, front_width = right_cols.shape
    slot_count = l_blocks.shape[4]
    solved_cols = jnp.zeros((levels * proc_rows, block_size, front_width), jnp.bfloat16)
    solutions = []
    for level in range(levels):
        right_part = right_cols[level].astype(jnp.float32)
        if level > 0:
            chosen = block_cols[level - 1, 0, 0]
            active = live_counts[level - 1, 0, 0]
            local_index = chosen // per_level * proc_rows + chosen % per_level // proc_cols
            live = jnp.arange(slot_count)[None, :] < active[:, None]
            masked = jnp.where(live[:, :, None, None], l_blocks[level - 1, 0, 0], jnp.zeros((), jnp.bfloat16))
            partial = jnp.einsum(
                "jkab,jkbr->jar", masked, solved_cols[local_index], preferred_element_type=jnp.float32
            ).astype(jnp.bfloat16)
            row_total = lax.psum_scatter(partial, "pcol", scatter_dimension=0, tiled=True)
            right_part = right_part - row_total[0].astype(jnp.float32)
        resid = right_part.astype(jnp.bfloat16)
        solved = jnp.dot(diag_inverse[level, 0, 0], resid, preferred_element_type=jnp.float32).astype(jnp.bfloat16)
        solutions.append(solved)
        if level + 1 < levels:
            segment = lax.all_gather(solved[None], "prow", axis=0, tiled=True)
            solved_cols = lax.dynamic_update_slice_in_dim(solved_cols, segment, level * proc_rows, 0)
    return jnp.stack(solutions)[:, None, None]


def first_kernel(n, m, place, counts_ref, cols_ref, b_ref, d_ref, full_ref, index_ref, own_ref, other_ref, away_ref, *refs):
    b_buf, d_buf, count_ref, col_ref, sems = refs
    middle = b_buf.shape[0]
    copies = [
        pltpu.make_async_copy(b_ref.at[0, 0, 0], b_buf.at[0], sems.at[0]),
        pltpu.make_async_copy(d_ref.at[0, 0, 0], d_buf.at[0], sems.at[1]),
        pltpu.make_async_copy(cols_ref, col_ref, sems.at[2]),
        pltpu.make_async_copy(counts_ref, count_ref, sems.at[3]),
        pltpu.make_async_copy(d_ref.at[pl.ds(1, middle - 1), 0, 0], d_buf.at[pl.ds(1, middle - 1)], sems.at[4]),
        pltpu.make_async_copy(b_ref.at[pl.ds(1, middle - 1), 0, 0], b_buf.at[pl.ds(1, middle - 1)], sems.at[5]),
    ]
    for copy in copies:
        copy.start()
    me, my_row, my_place = lax.axis_index("pcol"), lax.axis_index("prow"), place[0]
    for p in range(1, m):
        my_place = jnp.where(my_row == p, place[p], my_place)
    size, width = own_ref.shape
    for copy in copies[:2]:
        copy.wait()
    full_ref[...] = jnp.dot(d_buf[0], b_buf[0], preferred_element_type=jnp.float32).astype(jnp.bfloat16)
    own_ref[...] = full_ref[:, my_columns(me, width)]
    other_ref[...] = full_ref[:, my_columns(me ^ 1, width)]
    for copy in copies[2:]:
        copy.wait()
    for level in range(1, middle):
        at = (2 * level - 2) * size
        away_ref[at : at + size, :] = b_buf[level, :, my_columns(me ^ 1, width)]
        away_ref[at + size : at + 2 * size, :size] = d_buf[level]
        away_ref[at + size : at + 2 * size, size:] = jnp.zeros((size, width - size), jnp.bfloat16)
    levels, slots = col_ref.shape[0] + 1, col_ref.shape[-1]
    row_at = lax.broadcasted_iota(jnp.int32, (n, slots), 0)
    slot_at = lax.broadcasted_iota(jnp.int32, (n, slots), 1)
    index_ref[...] = jnp.zeros_like(index_ref)
    for level in range(1, levels):
        rest = col_ref[level - 1, 0, 0]
        first = jnp.zeros_like(rest)
        for _ in range(1, level):
            past = rest >= m * n
            first += jnp.where(past, m, 0)
            rest -= jnp.where(past, m * n, 0)
        ahead = place[0] - my_place + jnp.zeros_like(rest)
        for p in range(1, m):
            ahead += jnp.where(rest >= p * n, place[p] - place[p - 1], 0)
        entry = first + jnp.where(ahead < 0, ahead + m, ahead)
        count = jnp.zeros_like(rest)
        for q in range(n):
            count = jnp.where(row_at == q, count_ref[level - 1, 0, 0, q], count)
        index_ref[(level - 1) * n : level * n, :slots] = jnp.where(slot_at < count, entry, -1)


def my_columns(me, width):
    return pl.ds(pl.multiple_of((me & 1) * width, LANES), width)


def gather_kernel(n, level, m, early, late, *refs):
    index_refs, l_refs, refs = refs[:PAIR], refs[PAIR : 2 * PAIR], refs[2 * PAIR :]
    old_refs, refs = refs[: level - 1], refs[level - 1 :]
    x_refs, (total_ref, chosen_ref, known, own, sem) = refs[:-5], refs[-5:]
    copy = pltpu.make_async_copy(l_refs[0].at[level - 1, 0, 0], own, sem)
    copy.start()
    me = lax.axis_index("pcol")
    size, width = total_ref.shape[1:]
    slots = l_refs[0].shape[4]
    base = (level - 1) * m
    for back in range(level - 1):
        known[back * m : (back + 1) * m] = old_refs[back][...]
    for d, x_ref in zip(early, x_refs):
        known[base + d] = x_ref[...]
    none = jnp.zeros((size, width), jnp.bfloat16)
    no_block = jnp.zeros((size, size), jnp.bfloat16)
    for j in reversed(range(PAIR)):
        if j == 0:
            copy.wait()
        for jq in range(n):
            q = me ^ jq
            blocks, solved, chosen = [], [], [no_block] * len(late)
            for k in range(slots):
                entry = index_refs[j][(level - 1) * n + q, k]
                use = entry >= 0
                block = l_refs[j][level - 1, 0, 0, q, k] if j else own[q, k]
                for i, d in enumerate(late):
                    is_late = entry == base + d
                    use = jnp.logical_and(use, entry != base + d)
                    chosen[i] = jnp.where(is_late, block, chosen[i])
                blocks.append(block)
                solved.append(jnp.where(use, known[jnp.maximum(entry, 0), j], none))
            product = jnp.dot(
                jnp.concatenate(blocks, axis=1), jnp.concatenate(solved, axis=0), preferred_element_type=jnp.float32
            )
            total_ref[jq] = product if j == PAIR - 1 else total_ref[jq] + product
            for i in range(len(late)):
                at = (i * PAIR + j) * size
                chosen_ref[jq, :, at : at + size] = chosen[i]


def late_total(jq, total_ref, chosen_ref, panels):
    return total_ref[jq] + jnp.dot(chosen_ref[jq], panels, preferred_element_type=jnp.float32)


def late_panels(x_refs):
    return jnp.concatenate([x_ref[j] for x_ref in x_refs for j in range(PAIR)], axis=0)


def away_kernel(late, total_ref, chosen_ref, *refs):
    panels, out_refs = late_panels(refs[:late]), refs[late:]
    rows = out_refs[0].shape[0]
    for i, out_ref in enumerate(out_refs):
        for row in range(rows):
            out_ref[row] = late_total(PAIR + i * rows + row, total_ref, chosen_ref, panels).astype(jnp.bfloat16)


def stay_kernel(level, late, early, b_ref, d_ref, away_ref, total_ref, chosen_ref, *refs):
    x_refs, (right_ref, inverse_ref, panels_ref) = refs[: len(late) + len(early)], refs[len(late) + len(early) :]
    panels = late_panels(x_refs[: len(late)])
    size, width = right_ref.shape[1:]
    at = (2 * level - 2) * size
    for j in range(PAIR):
        total = late_total(j, total_ref, chosen_ref, panels)
        right = away_ref[at : at + size, :] if j else b_ref[level, 0, 0, :, my_columns(lax.axis_index("pcol"), width)]
        right_ref[j] = right.astype(jnp.float32) - total
        inverse_ref[j] = away_ref[at + size : at + 2 * size, :size] if j else d_ref[level, 0, 0]
    for d, x_ref in zip(late + early, x_refs):
        panels_ref[d] = x_ref[...]


def last_stay_kernel(late, b_ref, total_ref, chosen_ref, *refs):
    x_refs, (right_ref, send_ref) = refs[:late], refs[late:]
    panels = late_panels(x_refs)
    level, width = b_ref.shape[0] - 1, right_ref.shape[2]
    send_ref[...] = late_total(1, total_ref, chosen_ref, panels).astype(jnp.bfloat16)
    for j in range(PAIR):
        right_ref[j] = b_ref[level, 0, 0, :, my_columns(lax.axis_index("pcol") ^ j, width)].astype(jnp.float32)
    right_ref[0] = right_ref[0] - late_total(0, total_ref, chosen_ref, panels)


def solve_kernel(right_ref, inverse_ref, *refs):
    other_refs, out_ref = refs[:-1], refs[-1]
    for j in range(PAIR):
        resid = right_ref[j]
        for other in other_refs:
            resid -= other[j].astype(jnp.float32)
        value = jnp.dot(inverse_ref[j], resid.astype(jnp.bfloat16), preferred_element_type=jnp.float32)
        out_ref[j] = value.astype(jnp.bfloat16)


def write_kernel(full_ref, *refs):
    level_refs, (out_ref, sems) = refs[:-2], refs[-2:]
    width = level_refs[0].shape[2]
    copies = [pltpu.make_async_copy(full_ref, out_ref.at[0, 0, 0], sems.at[0])]
    for i, ref in enumerate(level_refs):
        target = out_ref.at[1 + i // PAIR, 0, 0, :, my_columns(lax.axis_index("pcol") ^ (i % PAIR), width)]
        copies.append(pltpu.make_async_copy(ref if i % PAIR else ref.at[0], target, sems.at[1 + i]))
    for copy in copies:
        copy.start()
    for copy in copies:
        copy.wait()


def last_kernel(d_ref, right_ref, mate_ref, *refs):
    other_refs, (_, out_ref, buf, sem) = refs[:-4], refs[-4:]
    width = right_ref.shape[2]
    levels = out_ref.shape[0]
    for j in range(PAIR):
        resid = right_ref[j]
        if j:
            resid -= mate_ref[...].astype(jnp.float32)
        for other in other_refs[j::PAIR]:
            resid -= other[0].astype(jnp.float32)
        value = jnp.dot(d_ref[levels - 1, 0, 0], resid.astype(jnp.bfloat16), preferred_element_type=jnp.float32)
        buf[:, my_columns(lax.axis_index("pcol") ^ j, width)] = value.astype(jnp.bfloat16)
    copy = pltpu.make_async_copy(buf, out_ref.at[levels - 1, 0, 0], sem)
    copy.start()
    copy.wait()


def after(value, *others):
    return lax.optimization_barrier((value, others))[0]


class Ring:
    def __init__(self, value, cycle):
        m = len(cycle)
        self.to_next = [(cycle[i], cycle[(i + 1) % m]) for i in range(m)]
        self.to_last = [(b, a) for a, b in self.to_next]
        self.size, self.step = m, 0
        self.found = {0: value}
        self.behind = self.ahead = value

    def advance(self):
        self.step += 1
        self.behind = lax.ppermute(self.behind, "prow", self.to_next)
        self.found[self.size - self.step] = self.behind
        if self.step < self.size - self.step:
            self.ahead = lax.ppermute(self.ahead, "prow", self.to_last)
            self.found[self.step] = self.ahead


def solve_paired(cycle, b_panels, diag_inverse, l_blocks, block_cols, live_counts):
    m = lax.axis_size("prow")
    n = lax.axis_size("pcol")
    levels, _, _, size, front = b_panels.shape
    slots = l_blocks.shape[4]
    width = front // PAIR
    place = [cycle.index(p) for p in range(m)]

    def send(value, bits):
        return lax.ppermute(value, "pcol", [(i, i ^ bits) for i in range(n)])

    index_shape = (-(-(levels - 1) * n // 8) * 8, LANES)

    middle = levels - 1

    full, index, own, other, away = pl.pallas_call(
        functools.partial(first_kernel, n, m, place),
        out_shape=[
            near((size, front)),
            near(index_shape, jnp.int32),
            near((size, width)),
            near((size, width)),
            near(((2 * middle - 2) * size, width)),
        ],
        in_specs=[anywhere()] * 4,
        out_specs=[vmem()] * 5,
        scratch_shapes=[
            pltpu.VMEM((middle, size, front), jnp.bfloat16),
            pltpu.VMEM((middle, size, size), jnp.bfloat16),
            pltpu.SMEM(live_counts.shape, jnp.int32),
            pltpu.VMEM(block_cols.shape, jnp.int32),
            pltpu.SemaphoreType.DMA((6,)),
        ],
        compiler_params=params(),
    )(*[in_hbm(v) for v in (live_counts, block_cols, b_panels, diag_inverse)])
    other, away, index = send(other, 1), send(away, 1), [index, send(index, 1)]
    solved = after(jnp.stack([own, other]), index[1])
    blocks = [in_hbm(l_blocks), send(after(l_blocks, solved), 1)]

    late = [m // 2 - 1, m // 2]
    early = [d for d in range(m) if d not in late]
    columns, kept = [], []
    for level in range(1, levels):
        final = level == levels - 1
        ring = Ring(solved, cycle)
        for step in range(m // 2):
            if level == 1 and step == 2:
                ring.ahead = after(ring.ahead, away)
            ring.advance()
        total, chosen = pl.pallas_call(
            functools.partial(gather_kernel, n, level, m, early, late),
            out_shape=[near((n, size, width), jnp.float32), near((n, size, len(late) * PAIR * size))],
            in_specs=[smem()] * PAIR + [anywhere()] + [vmem()] * (PAIR - 1 + len(kept) + len(early)),
            out_specs=[vmem()] * 2,
            scratch_shapes=[
                pltpu.VMEM((level * m, PAIR, size, width), jnp.bfloat16),
                pltpu.VMEM(l_blocks.shape[3:], jnp.bfloat16),
                pltpu.SemaphoreType.DMA,
            ],
            compiler_params=params(),
        )(*index, *blocks, *kept, *[ring.found[d] for d in early])
        rows = 1 if final else PAIR
        late_x, early_x = [ring.found[d] for d in late], [ring.found[d] for d in early]
        partial = pl.pallas_call(
            functools.partial(away_kernel, len(late)),
            out_shape=[near((rows, size, width))] * ((n - PAIR) // rows),
            in_specs=[vmem()] * (2 + len(late)),
            out_specs=[vmem()] * ((n - PAIR) // rows),
            compiler_params=params(),
        )(total, chosen, *late_x)
        others = [send(v, PAIR + rows * i) for i, v in enumerate(partial)]
        if final:
            columns = [v for solved in columns for v in (solved, send(after(solved, total)[1], 1))]
        total = after(total, partial)
        if final:
            break
        right, inverse, panels = pl.pallas_call(
            functools.partial(stay_kernel, level, late, early),
            out_shape=[
                near((PAIR, size, width), jnp.float32),
                near((PAIR, size, size)),
                near((m, PAIR, size, width)),
            ],
            in_specs=[vmem()] * (5 + m),
            out_specs=[vmem()] * 3,
            compiler_params=params(),
        )(b_panels, diag_inverse, away, total, chosen, *late_x, *early_x)
        kept.append(panels)
        solved = pl.pallas_call(
            solve_kernel,
            out_shape=near((PAIR, size, width)),
            in_specs=[vmem()] * (2 + len(others)),
            out_specs=vmem(),
            compiler_params=params(),
        )(right, inverse, *others)
        columns.append(solved)

    right, mate = pl.pallas_call(
        functools.partial(last_stay_kernel, len(late)),
        out_shape=[near((PAIR, size, width), jnp.float32), near((size, width))],
        in_specs=[vmem()] * (3 + len(late)),
        out_specs=[vmem()] * 2,
        compiler_params=params(),
    )(b_panels, total, chosen, *late_x)
    mate = send(after(mate, others[0]), 1)
    result = pl.pallas_call(
        write_kernel,
        out_shape=struct(b_panels.shape),
        in_specs=[vmem()] * (1 + len(columns)),
        out_specs=anywhere(),
        scratch_shapes=[pltpu.SemaphoreType.DMA((1 + len(columns),))],
        compiler_params=params(),
    )(full, *columns)
    return pl.pallas_call(
        last_kernel,
        out_shape=struct(b_panels.shape),
        in_specs=[vmem()] * (3 + len(others)) + [anywhere()],
        out_specs=anywhere(),
        scratch_shapes=[pltpu.VMEM((size, front), jnp.bfloat16), pltpu.SemaphoreType.DMA],
        input_output_aliases={3 + len(others): 0},
        compiler_params=params(),
    )(diag_inverse, right, mate, *others, result)


def cycle_of(mesh):
    m = mesh.shape["prow"]
    names = list(mesh.axis_names)
    devices = mesh.devices.transpose([names.index("prow"), names.index("pcol")])[:, 0]
    spots = [tuple(getattr(d, "coords", None) or (i, 0, 0)) for i, d in enumerate(devices)]

    def near(a, b):
        return sum(abs(u - v) for u, v in zip(spots[a], spots[b])) == 1

    def extend(path):
        if len(path) == m:
            return path if near(path[-1], path[0]) else None
        for p in range(m):
            if p not in path and near(path[-1], p):
                found = extend(path + [p])
                if found:
                    return found
        return None

    return extend([0]) or list(range(m))


def solution(mesh):
    n = mesh.shape["pcol"]
    cycle = cycle_of(mesh)

    def shards(b_panels, diag_inverse, l_blocks, block_cols, live_counts):
        front = b_panels.shape[-1]
        rows = mesh.shape["prow"]
        paired = n & (n - 1) == 0 and n >= PAIR and rows % 2 == 0 and rows > 2 and front % (PAIR * LANES) == 0
        paired = paired and n > PAIR and b_panels.shape[0] > 2 and front >= PAIR * b_panels.shape[-2]
        if paired and l_blocks.size * l_blocks.dtype.itemsize <= BLOCK_BYTES:
            return solve_paired(cycle, b_panels, diag_inverse, l_blocks, block_cols, live_counts)
        return solve_scattered(b_panels, diag_inverse, l_blocks, block_cols, live_counts)

    return jax.shard_map(
        shards,
        mesh=mesh,
        in_specs=(
            P(None, "prow", "pcol", None, None),
            P(None, "prow", "pcol", None, None),
            P(None, "prow", "pcol", None, None, None, None),
            P(None, "prow", "pcol", None, None),
            P(None, "prow", "pcol", None),
        ),
        out_specs=P(None, "prow", "pcol", None, None),
        check_vma=False,
    )
```

```python
import functools

import jax
import jax.numpy as jnp
from jax import lax
from jax.experimental import pallas as pl
from jax.experimental.pallas import tpu as pltpu
from jax.sharding import PartitionSpec as P

LANES = 128
PAIR = 2
BLOCK_BYTES = 4 * 2**20
VMEM_BYTES = 16 * 2**20


def vmem():
    return pl.BlockSpec(memory_space=pltpu.VMEM)


def smem():
    return pl.BlockSpec(memory_space=pltpu.SMEM)


def anywhere():
    return pl.BlockSpec(memory_space=pl.ANY)


def in_hbm(value):
    return pltpu.with_memory_space_constraint(value, pltpu.HBM)


def struct(shape, dtype=jnp.bfloat16):
    return jax.ShapeDtypeStruct(shape, dtype)


def near(shape, dtype=jnp.bfloat16):
    return pltpu.VMEM(shape, dtype)


def params():
    return pltpu.CompilerParams(vmem_limit_bytes=VMEM_BYTES)


def solve_scattered(b_panels, diag_inverse, l_blocks, block_cols, live_counts):
    proc_rows = lax.axis_size("prow")
    proc_cols = lax.axis_size("pcol")
    per_level = proc_rows * proc_cols
    right_cols = b_panels[:, 0, 0]
    levels, block_size, front_width = right_cols.shape
    slot_count = l_blocks.shape[4]
    solved_cols = jnp.zeros((levels * proc_rows, block_size, front_width), jnp.bfloat16)
    solutions = []
    for level in range(levels):
        right_part = right_cols[level].astype(jnp.float32)
        if level > 0:
            chosen = block_cols[level - 1, 0, 0]
            active = live_counts[level - 1, 0, 0]
            local_index = chosen // per_level * proc_rows + chosen % per_level // proc_cols
            live = jnp.arange(slot_count)[None, :] < active[:, None]
            masked = jnp.where(live[:, :, None, None], l_blocks[level - 1, 0, 0], jnp.zeros((), jnp.bfloat16))
            partial = jnp.einsum(
                "jkab,jkbr->jar", masked, solved_cols[local_index], preferred_element_type=jnp.float32
            ).astype(jnp.bfloat16)
            row_total = lax.psum_scatter(partial, "pcol", scatter_dimension=0, tiled=True)
            right_part = right_part - row_total[0].astype(jnp.float32)
        resid = right_part.astype(jnp.bfloat16)
        solved = jnp.dot(diag_inverse[level, 0, 0], resid, preferred_element_type=jnp.float32).astype(jnp.bfloat16)
        solutions.append(solved)
        if level + 1 < levels:
            segment = lax.all_gather(solved[None], "prow", axis=0, tiled=True)
            solved_cols = lax.dynamic_update_slice_in_dim(solved_cols, segment, level * proc_rows, 0)
    return jnp.stack(solutions)[:, None, None]


def first_kernel(n, m, place, counts_ref, cols_ref, b_ref, d_ref, full_ref, index_ref, own_ref, other_ref, away_ref, *refs):
    b_buf, d_buf, count_ref, col_ref, sems = refs
    middle = b_buf.shape[0]
    copies = [
        pltpu.make_async_copy(d_ref.at[0, 0, 0], d_buf.at[0], sems.at[4]),
        pltpu.make_async_copy(cols_ref, col_ref, sems.at[5]),
        pltpu.make_async_copy(counts_ref, count_ref, sems.at[6]),
        pltpu.make_async_copy(d_ref.at[pl.ds(1, middle - 1), 0, 0], d_buf.at[pl.ds(1, middle - 1)], sems.at[7]),
        pltpu.make_async_copy(b_ref.at[pl.ds(1, middle - 1), 0, 0], b_buf.at[pl.ds(1, middle - 1)], sems.at[8]),
    ]
    quarter = b_buf.shape[1] // 4
    first = [
        pltpu.make_async_copy(b_ref.at[0, 0, 0, pl.ds(i * quarter, quarter)], b_buf.at[0, pl.ds(i * quarter, quarter)], sems.at[i])
        for i in range(4)
    ]
    for copy in first + copies:
        copy.start()
    me, my_row, my_place = lax.axis_index("pcol"), lax.axis_index("prow"), place[0]
    for p in range(1, m):
        my_place = jnp.where(my_row == p, place[p], my_place)
    size, width = own_ref.shape
    for copy in first + copies[:1]:
        copy.wait()
    full_ref[...] = jnp.dot(d_buf[0], b_buf[0], preferred_element_type=jnp.float32).astype(jnp.bfloat16)
    own_ref[...] = full_ref[:, my_columns(me, width)]
    other_ref[...] = full_ref[:, my_columns(me ^ 1, width)]
    for copy in copies[1:]:
        copy.wait()
    for level in range(1, middle):
        at = (2 * level - 2) * size
        away_ref[at : at + size, :] = b_buf[level, :, my_columns(me ^ 1, width)]
        away_ref[at + size : at + 2 * size, :size] = d_buf[level]
        away_ref[at + size : at + 2 * size, size:] = jnp.zeros((size, width - size), jnp.bfloat16)
    levels, slots = col_ref.shape[0] + 1, col_ref.shape[-1]
    row_at = lax.broadcasted_iota(jnp.int32, (n, slots), 0)
    slot_at = lax.broadcasted_iota(jnp.int32, (n, slots), 1)
    index_ref[...] = jnp.zeros_like(index_ref)
    for level in range(1, levels):
        rest = col_ref[level - 1, 0, 0]
        first = jnp.zeros_like(rest)
        for _ in range(1, level):
            past = rest >= m * n
            first += jnp.where(past, m, 0)
            rest -= jnp.where(past, m * n, 0)
        ahead = place[0] - my_place + jnp.zeros_like(rest)
        for p in range(1, m):
            ahead += jnp.where(rest >= p * n, place[p] - place[p - 1], 0)
        entry = first + jnp.where(ahead < 0, ahead + m, ahead)
        count = jnp.zeros_like(rest)
        for q in range(n):
            count = jnp.where(row_at == q, count_ref[level - 1, 0, 0, q], count)
        index_ref[(level - 1) * n : level * n, :slots] = jnp.where(slot_at < count, entry, -1)


def my_columns(me, width):
    return pl.ds(pl.multiple_of((me & 1) * width, LANES), width)


def gather_kernel(n, level, m, early, late, *refs):
    index_refs, l_refs, refs = refs[:PAIR], refs[PAIR : 2 * PAIR], refs[2 * PAIR :]
    old_refs, refs = refs[: level - 1], refs[level - 1 :]
    x_refs, (total_ref, chosen_ref, known, own, sem) = refs[:-5], refs[-5:]
    copy = pltpu.make_async_copy(l_refs[0].at[level - 1, 0, 0], own, sem)
    copy.start()
    me = lax.axis_index("pcol")
    size, width = total_ref.shape[1:]
    slots = l_refs[0].shape[4]
    base = (level - 1) * m
    for back in range(level - 1):
        known[back * m : (back + 1) * m] = old_refs[back][...]
    for d, x_ref in zip(early, x_refs):
        known[base + d] = x_ref[...]
    none = jnp.zeros((size, width), jnp.bfloat16)
    no_block = jnp.zeros((size, size), jnp.bfloat16)
    for j in reversed(range(PAIR)):
        if j == 0:
            copy.wait()
        for jq in range(n):
            q = me ^ jq
            blocks, solved, chosen = [], [], [no_block] * len(late)
            for k in range(slots):
                entry = index_refs[j][(level - 1) * n + q, k]
                use = entry >= 0
                block = l_refs[j][level - 1, 0, 0, q, k] if j else own[q, k]
                for i, d in enumerate(late):
                    is_late = entry == base + d
                    use = jnp.logical_and(use, entry != base + d)
                    chosen[i] = jnp.where(is_late, block, chosen[i])
                blocks.append(block)
                solved.append(jnp.where(use, known[jnp.maximum(entry, 0), j], none))
            product = jnp.dot(
                jnp.concatenate(blocks, axis=1), jnp.concatenate(solved, axis=0), preferred_element_type=jnp.float32
            )
            total_ref[jq] = product if j == PAIR - 1 else total_ref[jq] + product
            for i in range(len(late)):
                at = (i * PAIR + j) * size
                chosen_ref[jq, :, at : at + size] = chosen[i]


def late_total(jq, total_ref, chosen_ref, panels):
    return total_ref[jq] + jnp.dot(chosen_ref[jq], panels, preferred_element_type=jnp.float32)


def late_panels(x_refs):
    return jnp.concatenate([x_ref[j] for x_ref in x_refs for j in range(PAIR)], axis=0)


def away_kernel(late, total_ref, chosen_ref, *refs):
    panels, out_refs = late_panels(refs[:late]), refs[late:]
    rows = out_refs[0].shape[0]
    for i, out_ref in enumerate(out_refs):
        for row in range(rows):
            out_ref[row] = late_total(PAIR + i * rows + row, total_ref, chosen_ref, panels).astype(jnp.bfloat16)


def stay_kernel(level, late, early, b_ref, d_ref, away_ref, total_ref, chosen_ref, *refs):
    x_refs, (right_ref, inverse_ref, panels_ref) = refs[: len(late) + len(early)], refs[len(late) + len(early) :]
    panels = late_panels(x_refs[: len(late)])
    size, width = right_ref.shape[1:]
    at = (2 * level - 2) * size
    for j in range(PAIR):
        total = late_total(j, total_ref, chosen_ref, panels)
        right = away_ref[at : at + size, :] if j else b_ref[level, 0, 0, :, my_columns(lax.axis_index("pcol"), width)]
        right_ref[j] = right.astype(jnp.float32) - total
        inverse_ref[j] = away_ref[at + size : at + 2 * size, :size] if j else d_ref[level, 0, 0]
    for d, x_ref in zip(late + early, x_refs):
        panels_ref[d] = x_ref[...]


def last_stay_kernel(late, b_ref, total_ref, chosen_ref, *refs):
    x_refs, (right_ref, send_ref) = refs[:late], refs[late:]
    panels = late_panels(x_refs)
    level, width = b_ref.shape[0] - 1, right_ref.shape[2]
    send_ref[...] = late_total(1, total_ref, chosen_ref, panels).astype(jnp.bfloat16)
    for j in range(PAIR):
        right_ref[j] = b_ref[level, 0, 0, :, my_columns(lax.axis_index("pcol") ^ j, width)].astype(jnp.float32)
    right_ref[0] = right_ref[0] - late_total(0, total_ref, chosen_ref, panels)


def solve_kernel(right_ref, inverse_ref, *refs):
    other_refs, out_ref = refs[:-1], refs[-1]
    for j in range(PAIR):
        resid = right_ref[j]
        for other in other_refs:
            resid -= other[j].astype(jnp.float32)
        value = jnp.dot(inverse_ref[j], resid.astype(jnp.bfloat16), preferred_element_type=jnp.float32)
        out_ref[j] = value.astype(jnp.bfloat16)


def write_kernel(full_ref, *refs):
    level_refs, (out_ref, sems) = refs[:-2], refs[-2:]
    width = level_refs[0].shape[2]
    copies = [pltpu.make_async_copy(full_ref, out_ref.at[0, 0, 0], sems.at[0])]
    for i, ref in enumerate(level_refs):
        target = out_ref.at[1 + i // PAIR, 0, 0, :, my_columns(lax.axis_index("pcol") ^ (i % PAIR), width)]
        copies.append(pltpu.make_async_copy(ref if i % PAIR else ref.at[0], target, sems.at[1 + i]))
    for copy in copies:
        copy.start()
    for copy in copies:
        copy.wait()


def last_kernel(d_ref, right_ref, mate_ref, *refs):
    other_refs, (_, out_ref, buf, sem) = refs[:-4], refs[-4:]
    width = right_ref.shape[2]
    levels = out_ref.shape[0]
    for j in range(PAIR):
        resid = right_ref[j]
        if j:
            resid -= mate_ref[...].astype(jnp.float32)
        for other in other_refs[j::PAIR]:
            resid -= other[0].astype(jnp.float32)
        value = jnp.dot(d_ref[levels - 1, 0, 0], resid.astype(jnp.bfloat16), preferred_element_type=jnp.float32)
        buf[:, my_columns(lax.axis_index("pcol") ^ j, width)] = value.astype(jnp.bfloat16)
    copy = pltpu.make_async_copy(buf, out_ref.at[levels - 1, 0, 0], sem)
    copy.start()
    copy.wait()


def after(value, *others):
    return lax.optimization_barrier((value, others))[0]


class Ring:
    def __init__(self, value, cycle):
        m = len(cycle)
        self.to_next = [(cycle[i], cycle[(i + 1) % m]) for i in range(m)]
        self.to_last = [(b, a) for a, b in self.to_next]
        self.size, self.step = m, 0
        self.found = {0: value}
        self.behind = self.ahead = value

    def advance(self):
        self.step += 1
        self.behind = lax.ppermute(self.behind, "prow", self.to_next)
        self.found[self.size - self.step] = self.behind
        if self.step < self.size - self.step:
            self.ahead = lax.ppermute(self.ahead, "prow", self.to_last)
            self.found[self.step] = self.ahead


def solve_paired(cycle, b_panels, diag_inverse, l_blocks, block_cols, live_counts):
    m = lax.axis_size("prow")
    n = lax.axis_size("pcol")
    levels, _, _, size, front = b_panels.shape
    slots = l_blocks.shape[4]
    width = front // PAIR
    place = [cycle.index(p) for p in range(m)]

    def send(value, bits):
        return lax.ppermute(value, "pcol", [(i, i ^ bits) for i in range(n)])

    index_shape = (-(-(levels - 1) * n // 8) * 8, LANES)

    middle = levels - 1

    full, index, own, other, away = pl.pallas_call(
        functools.partial(first_kernel, n, m, place),
        out_shape=[
            near((size, front)),
            near(index_shape, jnp.int32),
            near((size, width)),
            near((size, width)),
            near(((2 * middle - 2) * size, width)),
        ],
        in_specs=[anywhere()] * 4,
        out_specs=[vmem()] * 5,
        scratch_shapes=[
            pltpu.VMEM((middle, size, front), jnp.bfloat16),
            pltpu.VMEM((middle, size, size), jnp.bfloat16),
            pltpu.SMEM(live_counts.shape, jnp.int32),
            pltpu.VMEM(block_cols.shape, jnp.int32),
            pltpu.SemaphoreType.DMA((9,)),
        ],
        compiler_params=params(),
    )(*[in_hbm(v) for v in (live_counts, block_cols, b_panels, diag_inverse)])
    other, away, index = send(other, 1), send(away, 1), [index, send(index, 1)]
    solved = after(jnp.stack([own, other]), index[1])
    blocks = [in_hbm(l_blocks), send(after(l_blocks, solved), 1)]

    late = [m // 2 - 1, m // 2]
    early = [d for d in range(m) if d not in late]
    columns, kept = [], []
    for level in range(1, levels):
        final = level == levels - 1
        ring = Ring(solved, cycle)
        for step in range(m // 2):
            if level == 1 and step == 2:
                ring.ahead = after(ring.ahead, away)
            ring.advance()
        total, chosen = pl.pallas_call(
            functools.partial(gather_kernel, n, level, m, early, late),
            out_shape=[near((n, size, width), jnp.float32), near((n, size, len(late) * PAIR * size))],
            in_specs=[smem()] * PAIR + [anywhere()] + [vmem()] * (PAIR - 1 + len(kept) + len(early)),
            out_specs=[vmem()] * 2,
            scratch_shapes=[
                pltpu.VMEM((level * m, PAIR, size, width), jnp.bfloat16),
                pltpu.VMEM(l_blocks.shape[3:], jnp.bfloat16),
                pltpu.SemaphoreType.DMA,
            ],
            compiler_params=params(),
        )(*index, *blocks, *kept, *[ring.found[d] for d in early])
        rows = 1 if final else PAIR
        late_x, early_x = [ring.found[d] for d in late], [ring.found[d] for d in early]
        partial = pl.pallas_call(
            functools.partial(away_kernel, len(late)),
            out_shape=[near((rows, size, width))] * ((n - PAIR) // rows),
            in_specs=[vmem()] * (2 + len(late)),
            out_specs=[vmem()] * ((n - PAIR) // rows),
            compiler_params=params(),
        )(total, chosen, *late_x)
        others = [send(v, PAIR + rows * i) for i, v in enumerate(partial)]
        if final:
            columns = [v for solved in columns for v in (solved, send(after(solved, total)[1], 1))]
        total = after(total, partial)
        if final:
            break
        right, inverse, panels = pl.pallas_call(
            functools.partial(stay_kernel, level, late, early),
            out_shape=[
                near((PAIR, size, width), jnp.float32),
                near((PAIR, size, size)),
                near((m, PAIR, size, width)),
            ],
            in_specs=[vmem()] * (5 + m),
            out_specs=[vmem()] * 3,
            compiler_params=params(),
        )(b_panels, diag_inverse, away, total, chosen, *late_x, *early_x)
        kept.append(panels)
        solved = pl.pallas_call(
            solve_kernel,
            out_shape=near((PAIR, size, width)),
            in_specs=[vmem()] * (2 + len(others)),
            out_specs=vmem(),
            compiler_params=params(),
        )(right, inverse, *others)
        columns.append(solved)

    right, mate = pl.pallas_call(
        functools.partial(last_stay_kernel, len(late)),
        out_shape=[near((PAIR, size, width), jnp.float32), near((size, width))],
        in_specs=[vmem()] * (3 + len(late)),
        out_specs=[vmem()] * 2,
        compiler_params=params(),
    )(b_panels, total, chosen, *late_x)
    mate = send(after(mate, others[0]), 1)
    result = pl.pallas_call(
        write_kernel,
        out_shape=struct(b_panels.shape),
        in_specs=[vmem()] * (1 + len(columns)),
        out_specs=anywhere(),
        scratch_shapes=[pltpu.SemaphoreType.DMA((1 + len(columns),))],
        compiler_params=params(),
    )(full, *columns)
    return pl.pallas_call(
        last_kernel,
        out_shape=struct(b_panels.shape),
        in_specs=[vmem()] * (3 + len(others)) + [anywhere()],
        out_specs=anywhere(),
        scratch_shapes=[pltpu.VMEM((size, front), jnp.bfloat16), pltpu.SemaphoreType.DMA],
        input_output_aliases={3 + len(others): 0},
        compiler_params=params(),
    )(diag_inverse, right, mate, *others, result)


def cycle_of(mesh):
    m = mesh.shape["prow"]
    names = list(mesh.axis_names)
    devices = mesh.devices.transpose([names.index("prow"), names.index("pcol")])[:, 0]
    spots = [tuple(getattr(d, "coords", None) or (i, 0, 0)) for i, d in enumerate(devices)]

    def near(a, b):
        return sum(abs(u - v) for u, v in zip(spots[a], spots[b])) == 1

    def extend(path):
        if len(path) == m:
            return path if near(path[-1], path[0]) else None
        for p in range(m):
            if p not in path and near(path[-1], p):
                found = extend(path + [p])
                if found:
                    return found
        return None

    return extend([0]) or list(range(m))


def solution(mesh):
    n = mesh.shape["pcol"]
    cycle = cycle_of(mesh)

    def shards(b_panels, diag_inverse, l_blocks, block_cols, live_counts):
        front = b_panels.shape[-1]
        rows = mesh.shape["prow"]
        paired = n & (n - 1) == 0 and n >= PAIR and rows % 2 == 0 and rows > 2 and front % (PAIR * LANES) == 0
        paired = paired and b_panels.shape[-2] % 64 == 0 and n > PAIR and b_panels.shape[0] > 2 and front >= PAIR * b_panels.shape[-2]
        if paired and l_blocks.size * l_blocks.dtype.itemsize <= BLOCK_BYTES:
            return solve_paired(cycle, b_panels, diag_inverse, l_blocks, block_cols, live_counts)
        return solve_scattered(b_panels, diag_inverse, l_blocks, block_cols, live_counts)

    return jax.shard_map(
        shards,
        mesh=mesh,
        in_specs=(
            P(None, "prow", "pcol", None, None),
            P(None, "prow", "pcol", None, None),
            P(None, "prow", "pcol", None, None, None, None),
            P(None, "prow", "pcol", None, None),
            P(None, "prow", "pcol", None),
        ),
        out_specs=P(None, "prow", "pcol", None, None),
        check_vma=False,
    )
```

```python
import functools

import jax
import jax.numpy as jnp
from jax import lax
from jax.experimental import pallas as pl
from jax.experimental.pallas import tpu as pltpu
from jax.sharding import PartitionSpec as P

LANES = 128
PAIR = 2
BLOCK_BYTES = 4 * 2**20
VMEM_BYTES = 16 * 2**20


def vmem():
    return pl.BlockSpec(memory_space=pltpu.VMEM)


def smem():
    return pl.BlockSpec(memory_space=pltpu.SMEM)


def anywhere():
    return pl.BlockSpec(memory_space=pl.ANY)


def in_hbm(value):
    return pltpu.with_memory_space_constraint(value, pltpu.HBM)


def struct(shape, dtype=jnp.bfloat16):
    return jax.ShapeDtypeStruct(shape, dtype)


def near(shape, dtype=jnp.bfloat16):
    return pltpu.VMEM(shape, dtype)


def params():
    return pltpu.CompilerParams(vmem_limit_bytes=VMEM_BYTES)


def solve_scattered(b_panels, diag_inverse, l_blocks, block_cols, live_counts):
    proc_rows = lax.axis_size("prow")
    proc_cols = lax.axis_size("pcol")
    per_level = proc_rows * proc_cols
    right_cols = b_panels[:, 0, 0]
    levels, block_size, front_width = right_cols.shape
    slot_count = l_blocks.shape[4]
    solved_cols = jnp.zeros((levels * proc_rows, block_size, front_width), jnp.bfloat16)
    solutions = []
    for level in range(levels):
        right_part = right_cols[level].astype(jnp.float32)
        if level > 0:
            chosen = block_cols[level - 1, 0, 0]
            active = live_counts[level - 1, 0, 0]
            local_index = chosen // per_level * proc_rows + chosen % per_level // proc_cols
            live = jnp.arange(slot_count)[None, :] < active[:, None]
            masked = jnp.where(live[:, :, None, None], l_blocks[level - 1, 0, 0], jnp.zeros((), jnp.bfloat16))
            partial = jnp.einsum(
                "jkab,jkbr->jar", masked, solved_cols[local_index], preferred_element_type=jnp.float32
            ).astype(jnp.bfloat16)
            row_total = lax.psum_scatter(partial, "pcol", scatter_dimension=0, tiled=True)
            right_part = right_part - row_total[0].astype(jnp.float32)
        resid = right_part.astype(jnp.bfloat16)
        solved = jnp.dot(diag_inverse[level, 0, 0], resid, preferred_element_type=jnp.float32).astype(jnp.bfloat16)
        solutions.append(solved)
        if level + 1 < levels:
            segment = lax.all_gather(solved[None], "prow", axis=0, tiled=True)
            solved_cols = lax.dynamic_update_slice_in_dim(solved_cols, segment, level * proc_rows, 0)
    return jnp.stack(solutions)[:, None, None]


def first_kernel(n, m, place, counts_ref, cols_ref, b_ref, d_ref, index_ref, own_ref, other_ref, away_ref, *refs):
    b_buf, d_buf, count_ref, col_ref, sems = refs
    middle = b_buf.shape[0]
    copies = [
        pltpu.make_async_copy(b_ref.at[0, 0, 0], b_buf.at[0], sems.at[0]),
        pltpu.make_async_copy(d_ref.at[0, 0, 0], d_buf.at[0], sems.at[1]),
        pltpu.make_async_copy(cols_ref, col_ref, sems.at[2]),
        pltpu.make_async_copy(counts_ref, count_ref, sems.at[3]),
        pltpu.make_async_copy(d_ref.at[pl.ds(1, middle - 1), 0, 0], d_buf.at[pl.ds(1, middle - 1)], sems.at[4]),
        pltpu.make_async_copy(b_ref.at[pl.ds(1, middle - 1), 0, 0], b_buf.at[pl.ds(1, middle - 1)], sems.at[5]),
    ]
    for copy in copies:
        copy.start()
    me, my_row, my_place = lax.axis_index("pcol"), lax.axis_index("prow"), place[0]
    for p in range(1, m):
        my_place = jnp.where(my_row == p, place[p], my_place)
    size, width = own_ref.shape
    for copy in copies[:2]:
        copy.wait()
    for j, out_ref in enumerate((own_ref, other_ref)):
        value = jnp.dot(d_buf[0], b_buf[0, :, my_columns(me ^ j, width)], preferred_element_type=jnp.float32)
        out_ref[...] = value.astype(jnp.bfloat16)
    for copy in copies[2:]:
        copy.wait()
    for level in range(1, middle):
        at = (2 * level - 2) * size
        away_ref[at : at + size, :] = b_buf[level, :, my_columns(me ^ 1, width)]
        away_ref[at + size : at + 2 * size, :size] = d_buf[level]
        away_ref[at + size : at + 2 * size, size:] = jnp.zeros((size, width - size), jnp.bfloat16)
    levels, slots = col_ref.shape[0] + 1, col_ref.shape[-1]
    row_at = lax.broadcasted_iota(jnp.int32, (n, slots), 0)
    slot_at = lax.broadcasted_iota(jnp.int32, (n, slots), 1)
    index_ref[...] = jnp.zeros_like(index_ref)
    for level in range(1, levels):
        rest = col_ref[level - 1, 0, 0]
        first = jnp.zeros_like(rest)
        for _ in range(1, level):
            past = rest >= m * n
            first += jnp.where(past, m, 0)
            rest -= jnp.where(past, m * n, 0)
        ahead = place[0] - my_place + jnp.zeros_like(rest)
        for p in range(1, m):
            ahead += jnp.where(rest >= p * n, place[p] - place[p - 1], 0)
        entry = first + jnp.where(ahead < 0, ahead + m, ahead)
        count = jnp.zeros_like(rest)
        for q in range(n):
            count = jnp.where(row_at == q, count_ref[level - 1, 0, 0, q], count)
        index_ref[(level - 1) * n : level * n, :slots] = jnp.where(slot_at < count, entry, -1)


def my_columns(me, width):
    return pl.ds(pl.multiple_of((me & 1) * width, LANES), width)


def gather_kernel(n, level, m, early, late, *refs):
    index_refs, l_refs, refs = refs[:PAIR], refs[PAIR : 2 * PAIR], refs[2 * PAIR :]
    old_refs, refs = refs[: level - 1], refs[level - 1 :]
    x_refs, (total_ref, chosen_ref, known, own, sem) = refs[:-5], refs[-5:]
    copy = pltpu.make_async_copy(l_refs[0].at[level - 1, 0, 0], own, sem)
    copy.start()
    me = lax.axis_index("pcol")
    size, width = total_ref.shape[1:]
    slots = l_refs[0].shape[4]
    base = (level - 1) * m
    for back in range(level - 1):
        known[back * m : (back + 1) * m] = old_refs[back][...]
    for d, x_ref in zip(early, x_refs):
        known[base + d] = x_ref[...]
    none = jnp.zeros((size, width), jnp.bfloat16)
    no_block = jnp.zeros((size, size), jnp.bfloat16)
    for j in reversed(range(PAIR)):
        if j == 0:
            copy.wait()
        for jq in range(n):
            q = me ^ jq
            blocks, solved, chosen = [], [], [no_block] * len(late)
            for k in range(slots):
                entry = index_refs[j][(level - 1) * n + q, k]
                use = entry >= 0
                block = l_refs[j][level - 1, 0, 0, q, k] if j else own[q, k]
                for i, d in enumerate(late):
                    is_late = entry == base + d
                    use = jnp.logical_and(use, entry != base + d)
                    chosen[i] = jnp.where(is_late, block, chosen[i])
                blocks.append(block)
                solved.append(jnp.where(use, known[jnp.maximum(entry, 0), j], none))
            product = jnp.dot(
                jnp.concatenate(blocks, axis=1), jnp.concatenate(solved, axis=0), preferred_element_type=jnp.float32
            )
            total_ref[jq] = product if j == PAIR - 1 else total_ref[jq] + product
            for i in range(len(late)):
                at = (i * PAIR + j) * size
                chosen_ref[jq, :, at : at + size] = chosen[i]


def late_total(jq, total_ref, chosen_ref, panels):
    return total_ref[jq] + jnp.dot(chosen_ref[jq], panels, preferred_element_type=jnp.float32)


def late_panels(x_refs):
    return jnp.concatenate([x_ref[j] for x_ref in x_refs for j in range(PAIR)], axis=0)


def away_kernel(late, total_ref, chosen_ref, *refs):
    panels, out_refs = late_panels(refs[:late]), refs[late:]
    rows = out_refs[0].shape[0]
    for i, out_ref in enumerate(out_refs):
        for row in range(rows):
            out_ref[row] = late_total(PAIR + i * rows + row, total_ref, chosen_ref, panels).astype(jnp.bfloat16)


def stay_kernel(level, late, early, b_ref, d_ref, away_ref, total_ref, chosen_ref, *refs):
    x_refs, (right_ref, inverse_ref, panels_ref) = refs[: len(late) + len(early)], refs[len(late) + len(early) :]
    panels = late_panels(x_refs[: len(late)])
    size, width = right_ref.shape[1:]
    at = (2 * level - 2) * size
    for j in range(PAIR):
        total = late_total(j, total_ref, chosen_ref, panels)
        right = away_ref[at : at + size, :] if j else b_ref[level, 0, 0, :, my_columns(lax.axis_index("pcol"), width)]
        right_ref[j] = right.astype(jnp.float32) - total
        inverse_ref[j] = away_ref[at + size : at + 2 * size, :size] if j else d_ref[level, 0, 0]
    for d, x_ref in zip(late + early, x_refs):
        panels_ref[d] = x_ref[...]


def last_stay_kernel(late, b_ref, total_ref, chosen_ref, *refs):
    x_refs, (right_ref, send_ref) = refs[:late], refs[late:]
    panels = late_panels(x_refs)
    level, width = b_ref.shape[0] - 1, right_ref.shape[2]
    send_ref[...] = late_total(1, total_ref, chosen_ref, panels).astype(jnp.bfloat16)
    for j in range(PAIR):
        right_ref[j] = b_ref[level, 0, 0, :, my_columns(lax.axis_index("pcol") ^ j, width)].astype(jnp.float32)
    right_ref[0] = right_ref[0] - late_total(0, total_ref, chosen_ref, panels)


def solve_kernel(right_ref, inverse_ref, *refs):
    other_refs, out_ref = refs[:-1], refs[-1]
    for j in range(PAIR):
        resid = right_ref[j]
        for other in other_refs:
            resid -= other[j].astype(jnp.float32)
        value = jnp.dot(inverse_ref[j], resid.astype(jnp.bfloat16), preferred_element_type=jnp.float32)
        out_ref[j] = value.astype(jnp.bfloat16)


def write_kernel(*refs):
    piece_refs, (out_ref, sems) = refs[:-2], refs[-2:]
    width = piece_refs[0].shape[1]
    copies = []
    for i, ref in enumerate(piece_refs):
        target = out_ref.at[i // PAIR, 0, 0, :, my_columns(lax.axis_index("pcol") ^ (i % PAIR), width)]
        source = ref.at[0] if len(ref.shape) == 3 else ref
        copies.append(pltpu.make_async_copy(source, target, sems.at[i]))
    for copy in copies:
        copy.start()
    for copy in copies:
        copy.wait()


def last_kernel(d_ref, right_ref, mate_ref, *refs):
    other_refs, (_, out_ref, buf, sem) = refs[:-4], refs[-4:]
    width = right_ref.shape[2]
    levels = out_ref.shape[0]
    for j in range(PAIR):
        resid = right_ref[j]
        if j:
            resid -= mate_ref[...].astype(jnp.float32)
        for other in other_refs[j::PAIR]:
            resid -= other[0].astype(jnp.float32)
        value = jnp.dot(d_ref[levels - 1, 0, 0], resid.astype(jnp.bfloat16), preferred_element_type=jnp.float32)
        buf[:, my_columns(lax.axis_index("pcol") ^ j, width)] = value.astype(jnp.bfloat16)
    copy = pltpu.make_async_copy(buf, out_ref.at[levels - 1, 0, 0], sem)
    copy.start()
    copy.wait()


def after(value, *others):
    return lax.optimization_barrier((value, others))[0]


class Ring:
    def __init__(self, value, cycle):
        m = len(cycle)
        self.to_next = [(cycle[i], cycle[(i + 1) % m]) for i in range(m)]
        self.to_last = [(b, a) for a, b in self.to_next]
        self.size, self.step = m, 0
        self.found = {0: value}
        self.behind = self.ahead = value

    def advance(self):
        self.step += 1
        self.behind = lax.ppermute(self.behind, "prow", self.to_next)
        self.found[self.size - self.step] = self.behind
        if self.step < self.size - self.step:
            self.ahead = lax.ppermute(self.ahead, "prow", self.to_last)
            self.found[self.step] = self.ahead


def solve_paired(cycle, b_panels, diag_inverse, l_blocks, block_cols, live_counts):
    m = lax.axis_size("prow")
    n = lax.axis_size("pcol")
    levels, _, _, size, front = b_panels.shape
    slots = l_blocks.shape[4]
    width = front // PAIR
    place = [cycle.index(p) for p in range(m)]

    def send(value, bits):
        return lax.ppermute(value, "pcol", [(i, i ^ bits) for i in range(n)])

    index_shape = (-(-(levels - 1) * n // 8) * 8, LANES)

    middle = levels - 1

    index, own, other, away = pl.pallas_call(
        functools.partial(first_kernel, n, m, place),
        out_shape=[
            near(index_shape, jnp.int32),
            near((size, width)),
            near((size, width)),
            near(((2 * middle - 2) * size, width)),
        ],
        in_specs=[anywhere()] * 4,
        out_specs=[vmem()] * 4,
        scratch_shapes=[
            pltpu.VMEM((middle, size, front), jnp.bfloat16),
            pltpu.VMEM((middle, size, size), jnp.bfloat16),
            pltpu.SMEM(live_counts.shape, jnp.int32),
            pltpu.VMEM(block_cols.shape, jnp.int32),
            pltpu.SemaphoreType.DMA((6,)),
        ],
        compiler_params=params(),
    )(*[in_hbm(v) for v in (live_counts, block_cols, b_panels, diag_inverse)])
    first = [own, other]
    other, away, index = send(other, 1), send(away, 1), [index, send(index, 1)]
    solved = after(jnp.stack([own, other]), index[1])
    blocks = [in_hbm(l_blocks), send(after(l_blocks, solved), 1)]

    late = [m // 2 - 1, m // 2]
    early = [d for d in range(m) if d not in late]
    columns, kept = [], []
    for level in range(1, levels):
        final = level == levels - 1
        ring = Ring(solved, cycle)
        for step in range(m // 2):
            if level == 1 and step == 2:
                ring.ahead = after(ring.ahead, away)
            ring.advance()
        total, chosen = pl.pallas_call(
            functools.partial(gather_kernel, n, level, m, early, late),
            out_shape=[near((n, size, width), jnp.float32), near((n, size, len(late) * PAIR * size))],
            in_specs=[smem()] * PAIR + [anywhere()] + [vmem()] * (PAIR - 1 + len(kept) + len(early)),
            out_specs=[vmem()] * 2,
            scratch_shapes=[
                pltpu.VMEM((level * m, PAIR, size, width), jnp.bfloat16),
                pltpu.VMEM(l_blocks.shape[3:], jnp.bfloat16),
                pltpu.SemaphoreType.DMA,
            ],
            compiler_params=params(),
        )(*index, *blocks, *kept, *[ring.found[d] for d in early])
        rows = 1 if final else PAIR
        late_x, early_x = [ring.found[d] for d in late], [ring.found[d] for d in early]
        partial = pl.pallas_call(
            functools.partial(away_kernel, len(late)),
            out_shape=[near((rows, size, width))] * ((n - PAIR) // rows),
            in_specs=[vmem()] * (2 + len(late)),
            out_specs=[vmem()] * ((n - PAIR) // rows),
            compiler_params=params(),
        )(total, chosen, *late_x)
        others = [send(v, PAIR + rows * i) for i, v in enumerate(partial)]
        if final:
            columns = [v for solved in columns for v in (solved, send(after(solved, total)[1], 1))]
        total = after(total, partial)
        if final:
            break
        right, inverse, panels = pl.pallas_call(
            functools.partial(stay_kernel, level, late, early),
            out_shape=[
                near((PAIR, size, width), jnp.float32),
                near((PAIR, size, size)),
                near((m, PAIR, size, width)),
            ],
            in_specs=[vmem()] * (5 + m),
            out_specs=[vmem()] * 3,
            compiler_params=params(),
        )(b_panels, diag_inverse, away, total, chosen, *late_x, *early_x)
        kept.append(panels)
        solved = pl.pallas_call(
            solve_kernel,
            out_shape=near((PAIR, size, width)),
            in_specs=[vmem()] * (2 + len(others)),
            out_specs=vmem(),
            compiler_params=params(),
        )(right, inverse, *others)
        columns.append(solved)

    right, mate = pl.pallas_call(
        functools.partial(last_stay_kernel, len(late)),
        out_shape=[near((PAIR, size, width), jnp.float32), near((size, width))],
        in_specs=[vmem()] * (3 + len(late)),
        out_specs=[vmem()] * 2,
        compiler_params=params(),
    )(b_panels, total, chosen, *late_x)
    mate = send(after(mate, others[0]), 1)
    result = pl.pallas_call(
        write_kernel,
        out_shape=struct(b_panels.shape),
        in_specs=[vmem()] * (PAIR + len(columns)),
        out_specs=anywhere(),
        scratch_shapes=[pltpu.SemaphoreType.DMA((PAIR + len(columns),))],
        compiler_params=params(),
    )(*first, *columns)
    return pl.pallas_call(
        last_kernel,
        out_shape=struct(b_panels.shape),
        in_specs=[vmem()] * (3 + len(others)) + [anywhere()],
        out_specs=anywhere(),
        scratch_shapes=[pltpu.VMEM((size, front), jnp.bfloat16), pltpu.SemaphoreType.DMA],
        input_output_aliases={3 + len(others): 0},
        compiler_params=params(),
    )(diag_inverse, right, mate, *others, result)


def cycle_of(mesh):
    m = mesh.shape["prow"]
    names = list(mesh.axis_names)
    devices = mesh.devices.transpose([names.index("prow"), names.index("pcol")])[:, 0]
    spots = [tuple(getattr(d, "coords", None) or (i, 0, 0)) for i, d in enumerate(devices)]

    def near(a, b):
        return sum(abs(u - v) for u, v in zip(spots[a], spots[b])) == 1

    def extend(path):
        if len(path) == m:
            return path if near(path[-1], path[0]) else None
        for p in range(m):
            if p not in path and near(path[-1], p):
                found = extend(path + [p])
                if found:
                    return found
        return None

    return extend([0]) or list(range(m))


def solution(mesh):
    n = mesh.shape["pcol"]
    cycle = cycle_of(mesh)

    def shards(b_panels, diag_inverse, l_blocks, block_cols, live_counts):
        front = b_panels.shape[-1]
        rows = mesh.shape["prow"]
        paired = n & (n - 1) == 0 and n >= PAIR and rows % 2 == 0 and rows > 2 and front % (PAIR * LANES) == 0
        paired = paired and n > PAIR and b_panels.shape[0] > 2 and front >= PAIR * b_panels.shape[-2]
        if paired and l_blocks.size * l_blocks.dtype.itemsize <= BLOCK_BYTES:
            return solve_paired(cycle, b_panels, diag_inverse, l_blocks, block_cols, live_counts)
        return solve_scattered(b_panels, diag_inverse, l_blocks, block_cols, live_counts)

    return jax.shard_map(
        shards,
        mesh=mesh,
        in_specs=(
            P(None, "prow", "pcol", None, None),
            P(None, "prow", "pcol", None, None),
            P(None, "prow", "pcol", None, None, None, None),
            P(None, "prow", "pcol", None, None),
            P(None, "prow", "pcol", None),
        ),
        out_specs=P(None, "prow", "pcol", None, None),
        check_vma=False,
    )
```
